128 devices in a mesh: pair: 8 (over y, core), fold: 16 (over z, x).
Axes of the slice: x: 4, y: 4, z: 4, core: 2. Of those that a mesh axis runs over, the one named last changes fastest.
Arguments:
- amplitudes: bfloat16 [4, 80, 640, 640], P(None, 'pair', 'fold'), may hold values from -6 to 6
- cycle_block: bfloat16 [640, 80, 16, 640], P('fold', None, 'pair'), may hold values from -0.078125 to 0.078125
- occ_sizes: int32 [8], replicated, may hold values from 1 to 20, 80 in all
- vir_sizes: int32 [8], replicated, may hold values from 1 to 160, 640 in all
- window_i: int32 [4], replicated, may hold values from 0 to 79
- window_occ: int32 [16], replicated, may hold values from 0 to 79
Outputs:
- residual: bfloat16 [4, 640, 16, 640], P(None, 'fold', 'pair')
The draws below stay inside these ranges and needn't reach their ends.
Inputs may be any that keep to these rules, and one draw needn't show every extreme that they name: `occ_sizes`: the entries sum to 80. `vir_sizes`: the entries sum to 640.
All inputs are finite; a program needn't handle non-finite values.
Results may differ from the reference program's by a relative error of at most 0.001.
Values may be sent and summed in bfloat16 or wider, within the bound.
No kernel may reach another device: no remote copies, remote signals or barrier semaphores. Data moves between devices by JAX's collectives and lax.ppermute only.
A program may use at most 128 MiB of HBM per device.

```python
import math
import jax
import jax.numpy as jnp
import numpy as np
from jax import lax

V = 640
NK = 80
NI = 4
NJ = 16
IRREPS = 8


def with_ends(values, key, least, top_value):
    longest = values.shape.index(max(values.shape))
    spots = []
    for shift in (0, 1):
        where = [jax.random.randint(jax.random.fold_in(key, axis), (), 0, length) for axis, length in enumerate(values.shape)]
        where[longest] = (where[longest] + shift) % values.shape[longest]
        spots.append(tuple(where))
    return values.at[spots[0]].set(least).at[spots[1]].set(top_value)


def spiked(array, stream_key, source, target, blocks, factor):
    def block_of(dim):
        return (jnp.arange(array.shape[dim]) // (array.shape[dim] // blocks)).reshape((-1,) + (1,) * (array.ndim - 1 - dim))

    first = jax.random.permutation(stream_key, blocks)[block_of(target)]
    other_side = (block_of(target) + blocks // 2) % blocks
    return jnp.where((block_of(source) == first) | (block_of(source) == other_side), factor * array, array)


def shard_levels(own_key, shape, pieces, least, top_value):
    def one(position, parts):
        steps = jax.random.uniform(jax.random.fold_in(jax.random.fold_in(own_key, 6), position), (parts,), jnp.float32, least / len(pieces), top_value / len(pieces))
        return jnp.repeat(jnp.exp(steps), shape[position] // parts).reshape((-1,) + (1,) * (len(shape) - position - 1))

    factor_of = one(*pieces[0])
    for cut in pieces[1:]:
        factor_of = factor_of * one(*cut)
    return factor_of


def length_profile(amount, total, bound, slope):
    loads = [(1 << 20) // math.isqrt(grade ** slope) + 1 for grade in range(2, amount + 1)]
    spare, counts = total - bound - (amount - 1), [1] * (amount - 1)
    while spare > 0:
        free = [i for i in range(amount - 1) if counts[i] < bound]
        whole, remaining = sum([loads[i] for i in free]), spare
        for i in free:
            extra = min(bound - counts[i], max(1, remaining * loads[i] // whole), spare)
            counts[i] = counts[i] + extra
            spare = spare - extra
    return np.array([bound] + counts)


def uneven(rng, amount, total, limit, slope):
    if amount == 2:
        one = jax.random.randint(rng, (), max(1, total - limit), min(limit, total - 1) + 1)
        return jnp.stack([one, total - one])
    tallies = jnp.asarray(length_profile(amount, total, limit, slope), jnp.int32)
    pairs = (amount - 1) // 2
    giver, sink = tallies[1:1 + 2 * pairs:2], tallies[2:2 + 2 * pairs:2]
    slack = jnp.minimum(giver - 1, limit - sink)
    shifted = jax.random.randint(jax.random.fold_in(rng, 1), (pairs,), 0, 1 << 20) % (slack + 1)
    tallies = tallies.at[1:1 + 2 * pairs:2].set(giver - shifted).at[2:2 + 2 * pairs:2].set(sink + shifted)
    return tallies[jax.random.permutation(jax.random.fold_in(rng, 2), amount)]


def centred(own_key, dims, width, most, shards=(), kind=jnp.bfloat16):
    values = width * jax.random.normal(own_key, dims, jnp.float32)
    if shards:
        values = values * shard_levels(own_key, dims, shards, -0.22, 0.18)
    return jnp.clip(values, -most, most).astype(kind)


def noise_with(key, shape, deviation, reach, cuts, heavy, kind=jnp.bfloat16):
    drawn = deviation * jax.random.normal(key, shape, jnp.float32)
    if cuts:
        drawn = drawn * shard_levels(key, shape, cuts, -0.22, 0.18)
    return jnp.clip(spiked(drawn, jax.random.fold_in(key, 3), *heavy), -reach, reach).astype(kind)


def setup_inputs(seed: int = 0) -> dict:
    key_of = jax.random.split(jax.random.key(seed), 7)
    amplitudes = noise_with(key_of[0], (NI, NK, V, V), 1.0, 6.0, ((1, 8), (2, 16)), (3, 2, 16, 2.0))
    cycle_block = centred(key_of[1], (V, NK, NJ, V), (NK * V // 8) ** -0.5, 0.078125, ((0, 16), (2, 8)))
    occ_sizes = uneven(key_of[2], IRREPS, NK, NK // 4, 2).astype(jnp.int32)
    vir_sizes = uneven(key_of[3], IRREPS, V, V // 4, 2).astype(jnp.int32)
    window_i = with_ends(jax.random.randint(key_of[4], (NI,), 0, NK), jax.random.fold_in(key_of[4], 1), 0, NK - 1).astype(jnp.int32)
    window_occ = with_ends(jax.random.randint(key_of[5], (NJ,), 0, NK), jax.random.fold_in(key_of[5], 1), 0, NK - 1).astype(jnp.int32)
    return dict(amplitudes=amplitudes, cycle_block=cycle_block, occ_sizes=occ_sizes, vir_sizes=vir_sizes, window_i=window_i, window_occ=window_occ)


def irrep_labels(sizes, count):
    boundaries = jnp.cumsum(sizes).astype(jnp.int32)
    positions = jnp.arange(count, dtype=jnp.int32)
    return jnp.sum((positions[:, None] >= boundaries[None, :]).astype(jnp.int32), axis=1).astype(jnp.int32)


def reference(amplitudes, cycle_block, occ_sizes, vir_sizes, window_i, window_occ):
    occ_labels = irrep_labels(occ_sizes, NK)
    vir_labels = irrep_labels(vir_sizes, V)
    i_labels = occ_labels[window_i]
    amp_parity = jnp.bitwise_xor(
        jnp.bitwise_xor(i_labels[:, None, None, None], occ_labels[None, :, None, None]),
        jnp.bitwise_xor(vir_labels[None, None, :, None], vir_labels[None, None, None, :]))
    masked_amps = jnp.where(amp_parity == 0, amplitudes, jnp.zeros_like(amplitudes))
    left_matrix = jnp.transpose(masked_amps, (0, 2, 1, 3)).reshape(NI * V, NK * V)

    def one_column(column):
        column_slab = lax.dynamic_index_in_dim(cycle_block, column, 2, keepdims=False)
        j_label = occ_labels[window_occ[column]]
        parity = jnp.bitwise_xor(jnp.bitwise_xor(vir_labels[:, None, None], occ_labels[None, :, None]), jnp.bitwise_xor(j_label, vir_labels[None, None, :]))
        masked = jnp.where(parity == 0, column_slab, jnp.zeros_like(column_slab))
        right_matrix = jnp.transpose(masked, (1, 0, 2)).reshape(NK * V, V)
        return jnp.dot(left_matrix, right_matrix, preferred_element_type=jnp.float32).astype(jnp.bfloat16)

    results = lax.map(one_column, jnp.arange(NJ, dtype=jnp.int32))
    return jnp.transpose(results.reshape(NJ, NI, V, V), (1, 2, 0, 3))
```

```python
import jax
import jax.numpy as jnp
from jax import lax
from jax.sharding import PartitionSpec as P


def irrep_labels(sizes, count):
    order = jnp.arange(sizes.shape[0], dtype=jnp.int32)
    boundaries = jnp.sum(jnp.where(order[None, :] <= order[:, None], sizes[None, :], 0), axis=1)
    positions = jnp.arange(count, dtype=jnp.int32)
    return jnp.sum((positions[:, None] >= boundaries[None, :]).astype(jnp.int32), axis=1)


def label_lookup(orbitals, labels, count):
    matches = orbitals[:, None] == jnp.arange(count, dtype=jnp.int32)[None, :]
    return jnp.sum(jnp.where(matches, labels[None, :], 0), axis=1)


def body(amplitudes, cycle_block, occ_sizes, vir_sizes, window_i, window_occ):
    c_local = cycle_block.shape[0]
    occ_total = cycle_block.shape[1]
    j_local = cycle_block.shape[2]
    vir_total = cycle_block.shape[3]
    k_local = amplitudes.shape[1]
    a_rows = amplitudes.shape[2]
    occ_labels = irrep_labels(occ_sizes, occ_total)
    vir_labels = irrep_labels(vir_sizes, vir_total)
    c_labels = lax.dynamic_slice_in_dim(vir_labels, lax.axis_index("fold") * c_local, c_local)
    a_labels = lax.dynamic_slice_in_dim(vir_labels, lax.axis_index("fold") * a_rows, a_rows)
    k_labels = lax.dynamic_slice_in_dim(occ_labels, lax.axis_index("pair") * k_local, k_local)
    i_labels = label_lookup(window_i, occ_labels, occ_total)
    j_orbitals = lax.dynamic_slice_in_dim(window_occ, lax.axis_index("pair") * j_local, j_local)
    j_labels = label_lookup(j_orbitals, occ_labels, occ_total)
    amp_parity = jnp.bitwise_xor(
        jnp.bitwise_xor(i_labels[:, None, None, None], k_labels[None, :, None, None]),
        jnp.bitwise_xor(a_labels[None, None, :, None], vir_labels[None, None, None, :]),
    )
    masked_amps = jnp.where(amp_parity == 0, amplitudes, jnp.zeros_like(amplitudes))
    parity = jnp.bitwise_xor(
        jnp.bitwise_xor(c_labels[:, None, None, None], occ_labels[None, :, None, None]),
        jnp.bitwise_xor(j_labels[None, None, :, None], vir_labels[None, None, None, :]),
    )
    masked = jnp.where(parity == 0, cycle_block, jnp.zeros_like(cycle_block))
    relaid = lax.all_to_all(masked_amps, "fold", split_axis=3, concat_axis=2, tiled=True)
    gathered = lax.all_gather(relaid, "pair", axis=1, tiled=True)
    partial_sum = jnp.einsum(
        "ikac,ckjb->iajb", gathered, masked, preferred_element_type=jnp.float32
    )
    summed = lax.psum(partial_sum, "fold")
    a_local = vir_total // lax.axis_size("fold")
    own_share = lax.dynamic_slice_in_dim(summed, lax.axis_index("fold") * a_local, a_local, 1)
    return own_share.astype(jnp.bfloat16)


def solution(mesh):
    placed = (P(None, "pair", "fold", None), P("fold", None, "pair", None), P(), P(), P(), P())
    return jax.shard_map(
        body, mesh=mesh, in_specs=placed, out_specs=P(None, "fold", "pair", None), check_vma=False
    )
```

```python
import jax
import jax.numpy as jnp
from jax import lax
from jax.sharding import PartitionSpec as P

BF16, F32 = jnp.bfloat16, jnp.float32


def prefix_sums(sizes):
    order = jnp.arange(sizes.shape[0], dtype=jnp.int32)
    return jnp.sum(jnp.where(order[None, :] <= order[:, None], sizes[None, :], 0), axis=1)


def irrep_labels(sizes, count):
    ends = prefix_sums(sizes)
    positions = jnp.arange(count, dtype=jnp.int32)
    after = positions[:, None] >= ends[None, :]
    labels = jnp.sum(after.astype(jnp.int32), axis=1)
    places = positions - jnp.sum(jnp.where(after, sizes[None, :], 0), axis=1)
    return labels, places


def label_lookup(orbitals, labels, count):
    matches = orbitals[:, None] == jnp.arange(count, dtype=jnp.int32)[None, :]
    return jnp.sum(jnp.where(matches, labels[None, :], 0), axis=1)


def one_hot_rows(places, width):
    return (jnp.arange(width, dtype=jnp.int32)[:, None] == places[None, :]).astype(BF16)


def pick(x, spec, y):
    return jnp.einsum(spec, x, y, preferred_element_type=F32).astype(BF16)


def body(amplitudes, cycle_block, occ_sizes, vir_sizes, window_i, window_occ):
    irreps = occ_sizes.shape[0]
    n_fold, n_pair = lax.axis_size("fold"), lax.axis_size("pair")
    fold, pair = lax.axis_index("fold"), lax.axis_index("pair")
    c_local, occ_total, j_local, vir_total = cycle_block.shape
    n_i, k_local, a_local, _ = amplitudes.shape
    vmax, omax = vir_total // 4, occ_total // 4
    halves = n_pair // n_i
    a_part = a_local // halves

    occ, occ_place = irrep_labels(occ_sizes, occ_total)
    vir, vir_place = irrep_labels(vir_sizes, vir_total)
    to_place = one_hot_rows(vir_place, vmax)
    to_kappa = one_hot_rows(occ_place, omax)
    own_vir = lax.dynamic_slice_in_dim(vir, fold * c_local, c_local)
    k_own = lax.dynamic_slice_in_dim(occ, pair * k_local, k_local)
    i_labels = label_lookup(window_i, occ, occ_total)
    j_labels = label_lookup(lax.dynamic_slice_in_dim(window_occ, pair * j_local, j_local), occ, occ_total)

    x = i_labels[:, None, None] ^ k_own[None, :, None] ^ own_vir[None, None, :]
    masked = jnp.where(x[..., None] == vir, amplitudes, jnp.zeros_like(amplitudes))
    narrow = pick(masked, "ikac,tc->ikat", to_place)
    narrow = narrow.reshape(n_i, k_local, halves, a_part, vmax).transpose(0, 2, 1, 3, 4)
    narrow = narrow.reshape(n_pair, k_local, a_part, vmax)
    narrow = lax.all_to_all(narrow, "pair", split_axis=0, concat_axis=0, tiled=True)
    narrow = narrow.reshape(occ_total, a_part, vmax)

    i_mine = lax.dynamic_index_in_dim(i_labels, pair // halves, keepdims=False)
    a_mine = lax.dynamic_slice_in_dim(vir, fold * a_local + (pair % halves) * a_part, a_part)
    wide = pick(narrow, "kat,tc->akc", to_place)
    x = i_mine ^ occ[None, :, None] ^ a_mine[:, None, None] ^ vir[None, None, :]
    wide = jnp.where(x == 0, wide, jnp.zeros_like(wide))
    short = pick(to_kappa, "qk,akc->aqc", wide)
    short = short.reshape(a_part, omax, n_fold, c_local).transpose(2, 0, 1, 3)
    short = short.reshape(n_fold, a_part, omax * c_local)
    short = lax.all_to_all(short, "fold", split_axis=0, concat_axis=0, tiled=True)
    lhs = lax.all_gather(short, "pair", axis=0)

    x = own_vir[:, None, None] ^ occ[None, :, None] ^ j_labels[None, None, :]
    masked = jnp.where(x[..., None] == vir, cycle_block, jnp.zeros_like(cycle_block))
    rhs = pick(masked, "ckjb,tb->ckjt", to_place)
    classes = jnp.arange(irreps, dtype=jnp.int32)
    x = classes[:, None, None] == (occ[None, :, None] ^ own_vir[None, None, :])
    chosen = jnp.where(x[:, None], to_kappa[None, :, :, None], jnp.zeros((), BF16))
    rhs = pick(chosen, "rqkc,ckjt->rqcjt", rhs)
    rhs = rhs.reshape(irreps * omax * c_local, j_local * vmax)

    a_class = vir.reshape(n_fold, halves, a_part)
    row = i_labels[:, None, None, None] ^ a_class.transpose(1, 0, 2)[None]
    row = row.reshape(n_pair, n_fold, a_part)
    spread = jnp.where(
        row[..., None, None] == classes[:, None], lhs[:, :, :, None, :], jnp.zeros((), BF16)
    ).reshape(n_pair, n_fold, a_part, -1)
    partial_sum = jnp.einsum("pfak,kn->fpan", spread, rhs, preferred_element_type=F32)
    shares = lax.all_to_all(partial_sum, "fold", split_axis=0, concat_axis=0, tiled=True)
    total = jnp.sum(shares, axis=0).astype(BF16)
    total = total.reshape(n_i, a_local, j_local, vmax)
    spread_b = pick(total, "iajt,tb->iajb", to_place)
    x = i_labels[:, None, None] ^ own_vir[None, :, None] ^ j_labels[None, None, :]
    return jnp.where(x[..., None] == vir, spread_b, jnp.zeros_like(spread_b))


def solution(mesh):
    placed = (P(None, "pair", "fold", None), P("fold", None, "pair", None), P(), P(), P(), P())
    return jax.shard_map(
        body, mesh=mesh, in_specs=placed, out_specs=P(None, "fold", "pair", None), check_vma=False
    )
```

```python
import functools

import jax
import jax.numpy as jnp
from jax import lax
from jax.experimental import pallas as pl
from jax.experimental.pallas import tpu as pltpu
from jax.sharding import PartitionSpec as P

BF16, F32 = jnp.bfloat16, jnp.float32


def prefix_sums(sizes):
    order = jnp.arange(sizes.shape[0], dtype=jnp.int32)
    return jnp.sum(jnp.where(order[None, :] <= order[:, None], sizes[None, :], 0), axis=1)


def irrep_labels(sizes, count):
    ends = prefix_sums(sizes)
    positions = jnp.arange(count, dtype=jnp.int32)
    after = positions[:, None] >= ends[None, :]
    labels = jnp.sum(after.astype(jnp.int32), axis=1)
    places = positions - jnp.sum(jnp.where(after, sizes[None, :], 0), axis=1)
    return labels, places


def label_lookup(orbitals, labels, count):
    matches = orbitals[:, None] == jnp.arange(count, dtype=jnp.int32)[None, :]
    return jnp.sum(jnp.where(matches, labels[None, :], 0), axis=1)


def one_hot_rows(places, width):
    return (jnp.arange(width, dtype=jnp.int32)[:, None] == places[None, :]).astype(BF16)


def pick(x, spec, y):
    return jnp.einsum(spec, x, y, preferred_element_type=F32).astype(BF16)


def grouped_kernel(scalars, lhs, rhs, c_label, out, rows, block, total, *, irreps, halves, window, c_local):
    step = pl.program_id(0)
    groups, n_rows, depth = lhs.shape
    n_i, n_j, width = groups // halves, rhs.shape[1], rhs.shape[3]
    k_starts = n_i + 2
    bounds = k_starts + irreps

    def place(h, _):
        k = scalars[k_starts + (step ^ h)]
        odd = k % 2
        first = pl.multiple_of(k * c_local + odd * (c_local % 16), 16)
        chosen = c_label[...] == h.astype(F32).astype(BF16)
        for j in range(n_j):
            block[j] = jnp.where(chosen, rhs[odd, j, pl.ds(first, depth), :], block[j])
        return 0

    lax.fori_loop(scalars[n_i], scalars[n_i + 1] + 1, place, 0)

    spans = []
    for g in range(groups):
        at = bounds + (g % halves) * (irreps + 1) + (step ^ scalars[g // halves])
        low, high = scalars[at], scalars[at + 1]
        base = pl.multiple_of(jnp.minimum(low // 16 * 16, n_rows - window), 16)
        rows[g * window:(g + 1) * window, :] = lhs[g, pl.ds(base, window), :]
        spans.append((low, high, base))
    for j in range(n_j):
        product = jnp.dot(rows[...], block[j], preferred_element_type=F32)
        for g, (low, high, base) in enumerate(spans):
            piece = product[g * window:(g + 1) * window]
            row = base + lax.broadcasted_iota(jnp.int32, piece.shape, 0)
            own = (row >= low) & (row < high)
            lane = (g % halves * n_j + j) * width
            spot = (g // halves, pl.ds(base, window), slice(lane, lane + width))
            total[spot] = jnp.where(own, piece, total[spot])

    @pl.when(step == irreps - 1)
    def _():
        part = n_rows // out.shape[0]
        for f in range(out.shape[0]):
            for i in range(n_i):
                out[f, i * part:(i + 1) * part, :] = total[i, f * part:(f + 1) * part, :]


def grouped_product(scalars, lhs, rhs, c_label, n_fold, *, irreps, halves, window, c_local):
    groups, n_rows, depth = lhs.shape
    _, n_j, _, width = rhs.shape
    n_i = groups // halves
    out_shape = (n_fold, n_i * n_rows // n_fold, halves * n_j * width)
    whole = lambda shape: pl.BlockSpec(shape, lambda r, s: (0,) * len(shape))
    return pl.pallas_call(
        functools.partial(grouped_kernel, irreps=irreps, halves=halves, window=window, c_local=c_local),
        out_shape=jax.ShapeDtypeStruct(out_shape, F32),
        grid_spec=pltpu.PrefetchScalarGridSpec(
            num_scalar_prefetch=1,
            grid=(irreps,),
            in_specs=[whole(lhs.shape), whole(rhs.shape), whole(c_label.shape)],
            out_specs=whole(out_shape),
            scratch_shapes=[
                pltpu.VMEM((groups * window, depth), BF16),
                pltpu.VMEM((n_j, depth, width), BF16),
                pltpu.VMEM((n_i, n_rows, halves * n_j * width), F32),
            ],
        ),
        compiler_params=pltpu.CompilerParams(vmem_limit_bytes=56 * 2**20),
        cost_estimate=pl.CostEstimate(
            flops=2 * irreps * groups * window * depth * n_j * width, bytes_accessed=16 * 2**20, transcendentals=0
        ),
    )(scalars, lhs, rhs, c_label)


def body(amplitudes, cycle_block, occ_sizes, vir_sizes, window_i, window_occ):
    irreps = occ_sizes.shape[0]
    n_fold, n_pair = lax.axis_size("fold"), lax.axis_size("pair")
    fold, pair = lax.axis_index("fold"), lax.axis_index("pair")
    c_local, occ_total, j_local, vir_total = cycle_block.shape
    n_i, k_local, a_local, _ = amplitudes.shape
    vmax, omax = vir_total // 4, occ_total // 4
    halves = n_pair // n_i
    a_part = a_local // halves

    occ, occ_place = irrep_labels(occ_sizes, occ_total)
    vir, vir_place = irrep_labels(vir_sizes, vir_total)
    to_place = one_hot_rows(vir_place, vmax)
    to_kappa = one_hot_rows(occ_place, omax)
    own_vir = lax.dynamic_slice_in_dim(vir, fold * c_local, c_local)
    k_own = lax.dynamic_slice_in_dim(occ, pair * k_local, k_local)
    i_labels = label_lookup(window_i, occ, occ_total)
    j_labels = label_lookup(lax.dynamic_slice_in_dim(window_occ, pair * j_local, j_local), occ, occ_total)

    x = i_labels[:, None, None] ^ k_own[None, :, None] ^ own_vir[None, None, :]
    masked = jnp.where(x[..., None] == vir, amplitudes, jnp.zeros_like(amplitudes))
    narrow = pick(masked, "ikac,tc->ikat", to_place)
    narrow = narrow.reshape(n_i, k_local, halves, a_part, vmax).transpose(0, 2, 1, 3, 4)
    narrow = narrow.reshape(n_pair, k_local, a_part, vmax)
    narrow = lax.all_to_all(narrow, "pair", split_axis=0, concat_axis=0, tiled=True)
    narrow = narrow.reshape(occ_total, a_part, vmax)

    i_mine = lax.dynamic_index_in_dim(i_labels, pair // halves, keepdims=False)
    a_mine = lax.dynamic_slice_in_dim(vir, fold * a_local + (pair % halves) * a_part, a_part)
    wide = pick(narrow, "kat,tc->akc", to_place)
    x = i_mine ^ occ[None, :, None] ^ a_mine[:, None, None] ^ vir[None, None, :]
    wide = jnp.where(x == 0, wide, jnp.zeros_like(wide))
    short = pick(to_kappa, "qk,akc->aqc", wide)
    short = short.reshape(a_part, omax, n_fold, c_local).transpose(2, 0, 1, 3)
    short = short.reshape(n_fold, a_part, omax * c_local)
    short = lax.all_to_all(short, "fold", split_axis=0, concat_axis=0, tiled=True)
    short = short.reshape(n_fold * a_part, omax * c_local)
    lhs = lax.all_gather(short, "pair", axis=0)

    x = own_vir[:, None, None] ^ occ[None, :, None] ^ j_labels[None, None, :]
    masked = jnp.where(x[..., None] == vir, cycle_block, jnp.zeros_like(cycle_block))
    rhs = pick(masked, "ckjb,tb->jkct", to_place).reshape(j_local, occ_total * c_local, vmax)
    half = c_local % 16
    beyond = omax * c_local
    rhs = jnp.stack([
        jnp.pad(rhs, ((0, 0), (0, beyond + 16), (0, 0))),
        jnp.pad(rhs, ((0, 0), (half, beyond + 16 - half), (0, 0))),
    ])
    c_label = jnp.tile(own_vir.astype(F32)[:, None], (omax, vmax)).astype(BF16)

    starts = jnp.concatenate([jnp.zeros((1,), jnp.int32), prefix_sums(vir_sizes)])
    inside = starts % a_local
    bounds = [starts // a_local * a_part + jnp.clip(inside - h * a_part, 0, a_part) for h in range(halves)]
    k_starts = prefix_sums(occ_sizes) - occ_sizes
    scalars = jnp.concatenate([i_labels, own_vir[:1], own_vir[-1:], k_starts] + bounds).astype(jnp.int32)
    most = min(vmax, -(-vmax // a_local) * a_part)
    window = min(-(-(most + 15) // 16) * 16, n_fold * a_part)
    partial_sum = grouped_product(
        scalars, lhs, rhs, c_label, n_fold, irreps=irreps, halves=halves, window=window, c_local=c_local
    )
    shares = lax.all_to_all(partial_sum, "fold", split_axis=0, concat_axis=0, tiled=True)
    total = jnp.sum(shares, axis=0).astype(BF16).reshape(n_i, a_part, halves, j_local, vmax)
    total = total.transpose(0, 2, 1, 3, 4).reshape(n_i, a_local, j_local, vmax)
    spread_b = pick(total, "iajt,tb->iajb", to_place)
    x = i_labels[:, None, None] ^ own_vir[None, :, None] ^ j_labels[None, None, :]
    return jnp.where(x[..., None] == vir, spread_b, jnp.zeros_like(spread_b))


def solution(mesh):
    placed = (P(None, "pair", "fold", None), P("fold", None, "pair", None), P(), P(), P(), P())
    return jax.shard_map(
        body, mesh=mesh, in_specs=placed, out_specs=P(None, "fold", "pair", None), check_vma=False
    )
```

```python
import functools
import math

import jax
import jax.numpy as jnp
from jax import lax
from jax.experimental import pallas as pl
from jax.experimental.pallas import tpu as pltpu
from jax.sharding import PartitionSpec as P

BF16, F32 = jnp.bfloat16, jnp.float32


def irrep_labels(sizes, count):
    positions = jnp.arange(count, dtype=jnp.int32)
    starts = [jnp.int32(0)]
    for g in range(sizes.shape[0]):
        starts.append(starts[-1] + sizes[g])
    labels, opened = jnp.zeros_like(positions), jnp.zeros_like(positions)
    for g in range(1, sizes.shape[0] + 1):
        after = positions >= starts[g]
        labels = jnp.where(after, g, labels)
        opened = jnp.where(after, starts[g], opened)
    return labels, positions - opened, jnp.stack(starts)


def label_lookup(orbitals, labels, count):
    matches = orbitals[:, None] == jnp.arange(count, dtype=jnp.int32)[None, :]
    return jnp.sum(jnp.where(matches, labels[None, :], 0), axis=1)


def one_hot_rows(places, width):
    return (jnp.arange(width, dtype=jnp.int32)[:, None] == places[None, :]).astype(BF16)


def pick(x, spec, y):
    return jnp.einsum(spec, x, y, preferred_element_type=F32).astype(BF16)


def block_kernel(scalars, cycle, c_label, code, out, chosen, picks, *, n_i, irreps, width):
    step = pl.program_id(0)
    n_j = cycle.shape[0]
    depth, vir_total = c_label.shape[0], cycle.shape[2]
    lane = lax.broadcasted_iota(jnp.int32, (vir_total, n_j * width), 1)
    for j in range(n_j):
        wanted = (step ^ scalars[n_i + 2 + irreps + j]) * width + lane - j * width
        own = (lane >= j * width) & (lane < (j + 1) * width) & (code[...] == wanted)
        picks[j * vir_total:(j + 1) * vir_total, :] = own.astype(F32).astype(BF16)

    def place(h, _):
        first = pl.multiple_of(scalars[n_i + 2 + (step ^ h)], 16)
        label = h.astype(F32).astype(BF16)
        for j in range(n_j):
            for at in range(0, vir_total, c_label.shape[1]):
                lanes = slice(at, at + c_label.shape[1])
                spot = slice(j * vir_total + at, j * vir_total + at + c_label.shape[1])
                chosen[:, spot] = jnp.where(
                    c_label[...] == label, cycle[j, pl.ds(first, depth), lanes], chosen[:, spot]
                )
        return 0

    lax.fori_loop(scalars[n_i], scalars[n_i + 1] + 1, place, 0)
    out[0] = jnp.dot(chosen[...], picks[...], preferred_element_type=F32).astype(BF16)


def class_blocks(scalars, cycle, c_label, code, *, n_i, irreps, width):
    n_j, _, vir_total = cycle.shape
    depth = c_label.shape[0]
    return pl.pallas_call(
        functools.partial(block_kernel, n_i=n_i, irreps=irreps, width=width),
        out_shape=jax.ShapeDtypeStruct((irreps, depth, n_j * width), BF16),
        grid_spec=pltpu.PrefetchScalarGridSpec(
            num_scalar_prefetch=1,
            grid=(irreps,),
            in_specs=[whole(cycle.shape), whole(c_label.shape), whole(code.shape)],
            out_specs=pl.BlockSpec((1, depth, n_j * width), lambda r, s: (r, 0, 0)),
            scratch_shapes=[
                pltpu.VMEM((depth, n_j * vir_total), BF16),
                pltpu.VMEM((n_j * vir_total, n_j * width), BF16),
            ],
        ),
        compiler_params=pltpu.CompilerParams(vmem_limit_bytes=48 * 2**20),
        cost_estimate=pl.CostEstimate(
            flops=2 * irreps * depth * n_j * vir_total * n_j * width, bytes_accessed=14 * 2**20, transcendentals=0
        ),
    )(scalars, cycle, c_label, code)


def grouped_kernel(scalars, lhs, block, first, second, rows, total, *, bounds, irreps, halves, window, side):
    step = pl.program_id(0)
    groups, n_rows, _ = lhs.shape
    n_i, width = groups // halves, block.shape[2]
    spans = []
    for g in range(groups):
        at = bounds + (g % halves) * (irreps + 1) + (step ^ scalars[g // halves])
        low, high = scalars[at], scalars[at + 1]
        base = pl.multiple_of(jnp.minimum(low // 16 * 16, n_rows - window), 16)
        rows[g * window:(g + 1) * window, :] = lhs[g, pl.ds(base, window), :]
        spans.append((low, high, base))
    product = jnp.dot(rows[...], block[0], preferred_element_type=F32)
    for g, (low, high, base) in enumerate(spans):
        piece = product[g * window:(g + 1) * window]
        row = base + lax.broadcasted_iota(jnp.int32, piece.shape, 0)
        spot = (g, pl.ds(base, window), slice(None))
        total[spot] = jnp.where((row >= low) & (row < high), piece, total[spot])

    @pl.when(step == irreps - 1)
    def _():
        n_fold = side[0] * side[1]
        part = n_rows // n_fold
        z, x = scalars[bounds - 2], scalars[bounds - 1]
        for f in range(n_fold):
            dz = lax.rem(f // side[1] - z + side[0], side[0])
            dx = lax.rem(f % side[1] - x + side[1], side[1])
            for g in range(groups):
                i, lane = g // halves, g % halves * width
                at = (i % (n_i // 2)) * part
                out, spot = (first, (dz, dx)) if i < n_i // 2 else (second, (dx, dz))
                out[spot + (slice(at, at + part), slice(lane, lane + width))] = total[g, f * part:(f + 1) * part, :]


def whole(shape):
    return pl.BlockSpec(shape, lambda r, s: (0,) * len(shape))


def grouped_product(scalars, lhs, block, *, bounds, irreps, halves, window, side):
    groups, n_rows, depth = lhs.shape
    width = block.shape[2]
    n_i = groups // halves
    tail = (n_i // 2 * n_rows // (side[0] * side[1]), halves * width)
    shapes = [(side[0], side[1]) + tail, (side[1], side[0]) + tail]
    return pl.pallas_call(
        functools.partial(
            grouped_kernel, bounds=bounds, irreps=irreps, halves=halves, window=window, side=side
        ),
        out_shape=[jax.ShapeDtypeStruct(shape, F32) for shape in shapes],
        grid_spec=pltpu.PrefetchScalarGridSpec(
            num_scalar_prefetch=1,
            grid=(irreps,),
            in_specs=[whole(lhs.shape), pl.BlockSpec((1, depth, width), lambda r, s: (r, 0, 0))],
            out_specs=[whole(shape) for shape in shapes],
            scratch_shapes=[pltpu.VMEM((groups * window, depth), BF16), pltpu.VMEM((groups, n_rows, width), F32)],
        ),
        compiler_params=pltpu.CompilerParams(vmem_limit_bytes=48 * 2**20),
        cost_estimate=pl.CostEstimate(
            flops=2 * irreps * groups * window * depth * width, bytes_accessed=13 * 2**20, transcendentals=0
        ),
    )(scalars, lhs, block)


def ring(side, along, step):
    pairs = []
    for z in range(side[0]):
        for x in range(side[1]):
            to = ((z + step) % side[0], x) if along == 0 else (z, (x + step) % side[1])
            pairs.append((z * side[1] + x, to[0] * side[1] + to[1]))
    return pairs


def ring_sums(parts, side, alongs):
    def send(v, along, step):
        return lax.ppermute(v, "fold", ring(side, along, step))

    halfway = [p.shape[1] // 2 if p.ndim > 3 else -(-p.shape[1] // 16) * 8 for p in parts]
    up = [send(p[2, :h], a, 1) for p, h, a in zip(parts, halfway, alongs)]
    down = [send(p[2, h:], a, -1) for p, h, a in zip(parts, halfway, alongs)]
    sums = []
    for p, u, d, h, a in zip(parts, up, down, halfway, alongs):
        right = send(jnp.concatenate([p[1, :h] + u, p[1, h:]]), a, 1)
        left = send(jnp.concatenate([p[3, :h], p[3, h:] + d]), a, -1)
        sums.append((p[0], right, left))
    return [p + r + l for p, r, l in sums]


def body(amplitudes, cycle_block, occ_sizes, vir_sizes, window_i, window_occ):
    irreps = occ_sizes.shape[0]
    n_fold, n_pair = lax.axis_size("fold"), lax.axis_size("pair")
    fold, pair = lax.axis_index("fold"), lax.axis_index("pair")
    c_local, occ_total, j_local, vir_total = cycle_block.shape
    n_i, k_local, a_local, _ = amplitudes.shape
    vmax, omax = vir_total // 4, occ_total // 4
    halves = n_pair // n_i
    a_part = a_local // halves

    occ, _, occ_starts = irrep_labels(occ_sizes, occ_total)
    vir, vir_place, starts = irrep_labels(vir_sizes, vir_total)
    to_place = one_hot_rows(vir_place, vmax)
    kappas = omax + 2 - omax % 2
    k_from = jnp.minimum(occ_starts[:irreps] // 2 * 2, occ_total - kappas)
    kappa = jnp.arange(occ_total, dtype=jnp.int32)
    for g in range(irreps):
        kappa = kappa - jnp.where(occ == g, k_from[g], 0)
    to_kappa = one_hot_rows(kappa, kappas)
    own_vir = lax.dynamic_slice_in_dim(vir, fold * c_local, c_local)
    k_own = lax.dynamic_slice_in_dim(occ, pair * k_local, k_local)
    i_labels = label_lookup(window_i, occ, occ_total)
    j_labels = label_lookup(lax.dynamic_slice_in_dim(window_occ, pair * j_local, j_local), occ, occ_total)

    x = i_labels[:, None, None] ^ k_own[None, :, None] ^ own_vir[None, None, :]
    masked = jnp.where(x[..., None] == vir, amplitudes, jnp.zeros_like(amplitudes))
    narrow = pick(masked, "ikac,tc->ikat", to_place)
    narrow = narrow.reshape(n_i, k_local, halves, a_part, vmax).transpose(0, 2, 1, 3, 4)
    narrow = narrow.reshape(n_pair, k_local, a_part, vmax)
    narrow = lax.all_to_all(narrow, "pair", split_axis=0, concat_axis=0, tiled=True)
    narrow = narrow.reshape(occ_total, a_part, vmax)

    i_mine = lax.dynamic_index_in_dim(i_labels, pair // halves, keepdims=False)
    a_mine = lax.dynamic_slice_in_dim(vir, fold * a_local + (pair % halves) * a_part, a_part)
    wide = pick(narrow, "kat,tc->akc", to_place)
    x = i_mine ^ occ[None, :, None] ^ a_mine[:, None, None] ^ vir[None, None, :]
    wide = jnp.where(x == 0, wide, jnp.zeros_like(wide))
    short = pick(to_kappa, "qk,akc->aqc", wide)
    short = short.reshape(a_part, kappas, n_fold, c_local).transpose(2, 0, 1, 3)
    short = short.reshape(n_fold, a_part, kappas * c_local)
    short = lax.all_to_all(short, "fold", split_axis=0, concat_axis=0, tiled=True)
    short = short.reshape(n_fold * a_part, kappas * c_local)
    lhs = lax.all_gather(short, "pair", axis=0)

    side = (4, 4) if n_fold == 16 else (n_fold, 1)
    inside = starts % a_local
    bounds = [starts // a_local * a_part + jnp.clip(inside - h * a_part, 0, a_part) for h in range(halves)]
    scalars = jnp.concatenate(
        [i_labels, own_vir[:1], own_vir[-1:], k_from * c_local, j_labels]
        + [jnp.stack([fold // side[1], fold % side[1]])] + bounds
    ).astype(jnp.int32)
    cycle = cycle_block.transpose(2, 1, 0, 3).reshape(j_local, occ_total * c_local, vir_total)
    lanes = math.gcd(vir_total, 128)
    c_label = jnp.tile(own_vir.astype(F32)[:, None], (kappas, lanes)).astype(BF16)
    code = jnp.broadcast_to((vir * vmax + vir_place)[:, None], (vir_total, j_local * vmax))
    blocks = class_blocks(scalars, cycle, c_label, code, n_i=n_i, irreps=irreps, width=vmax)

    most = min(vmax, -(-vmax // a_local) * a_part)
    window = min(-(-(most + 15) // 16) * 16, n_fold * a_part)
    first, second = grouped_product(
        scalars, lhs, blocks, bounds=n_i + irreps + j_local + 4, irreps=irreps, halves=halves, window=window, side=side
    )
    if side == (4, 4):
        first, second = ring_sums([first, second], side, (0, 1))
        first, second = ring_sums([first, second], side, (1, 0))
    else:
        order = lax.rem(jnp.arange(n_fold) - fold + n_fold, n_fold)
        both = jnp.concatenate([first[:, 0][order], second[0][order]], axis=1)
        shares = jnp.sum(lax.all_to_all(both, "fold", split_axis=0, concat_axis=0, tiled=True), axis=0)
        first, second = jnp.split(shares, 2)
    total = jnp.concatenate([first, second]).astype(BF16).reshape(n_i, a_part, halves, j_local, vmax)
    total = total.transpose(0, 2, 1, 3, 4).reshape(n_i, a_local, j_local, vmax)
    spread_b = pick(total, "iajt,tb->iajb", to_place)
    x = i_labels[:, None, None] ^ own_vir[None, :, None] ^ j_labels[None, None, :]
    return jnp.where(x[..., None] == vir, spread_b, jnp.zeros_like(spread_b))


def solution(mesh):
    placed = (P(None, "pair", "fold", None), P("fold", None, "pair", None), P(), P(), P(), P())
    return jax.shard_map(
        body, mesh=mesh, in_specs=placed, out_specs=P(None, "fold", "pair", None), check_vma=False
    )
```

```python
import functools
import math

import jax
import jax.numpy as jnp
from jax import lax
from jax.experimental import pallas as pl
from jax.experimental.pallas import tpu as pltpu
from jax.sharding import PartitionSpec as P

BF16, F32 = jnp.bfloat16, jnp.float32
TOP = 32767.0


def irrep_labels(sizes, count):
    order = jnp.arange(sizes.shape[0], dtype=jnp.int32)
    positions = jnp.arange(count, dtype=jnp.int32)
    ends = jnp.sum(jnp.where(order[None, :] <= order[:, None], sizes[None, :], 0), axis=1)
    after = positions[:, None] >= ends[None, :]
    labels = jnp.sum(after.astype(jnp.int32), axis=1)
    places = positions - jnp.sum(jnp.where(after, sizes[None, :], 0), axis=1)
    return labels, places, jnp.concatenate([jnp.zeros((1,), jnp.int32), ends])


def label_lookup(orbitals, labels, count):
    matches = orbitals[:, None] == jnp.arange(count, dtype=jnp.int32)[None, :]
    return jnp.sum(jnp.where(matches, labels[None, :], 0), axis=1)


def one_hot_rows(places, width):
    return (jnp.arange(width, dtype=jnp.int32)[:, None] == places[None, :]).astype(BF16)


def pick(x, spec, y):
    return jnp.einsum(spec, x, y, preferred_element_type=F32).astype(BF16)


def block_kernel(scalars, cycle, c_label, code, out, chosen, picks, *, n_i, irreps, width):
    step = pl.program_id(0)
    n_j = cycle.shape[0]
    depth, vir_total = c_label.shape[0], cycle.shape[2]
    lane = lax.broadcasted_iota(jnp.int32, (vir_total, n_j * width), 1)
    for j in range(n_j):
        wanted = (step ^ scalars[n_i + 2 + irreps + j]) * width + lane - j * width
        own = (lane >= j * width) & (lane < (j + 1) * width) & (code[...] == wanted)
        picks[j * vir_total:(j + 1) * vir_total, :] = own.astype(F32).astype(BF16)

    def place(h, _):
        first = pl.multiple_of(scalars[n_i + 2 + (step ^ h)], 16)
        label = h.astype(F32).astype(BF16)
        for j in range(n_j):
            for at in range(0, vir_total, c_label.shape[1]):
                lanes = slice(at, at + c_label.shape[1])
                spot = slice(j * vir_total + at, j * vir_total + at + c_label.shape[1])
                chosen[:, spot] = jnp.where(
                    c_label[...] == label, cycle[j, pl.ds(first, depth), lanes], chosen[:, spot]
                )
        return 0

    lax.fori_loop(scalars[n_i], scalars[n_i + 1] + 1, place, 0)
    out[0] = jnp.dot(chosen[...], picks[...], preferred_element_type=F32).astype(BF16)


def class_blocks(scalars, cycle, c_label, code, *, n_i, irreps, width):
    n_j, _, vir_total = cycle.shape
    depth = c_label.shape[0]
    return pl.pallas_call(
        functools.partial(block_kernel, n_i=n_i, irreps=irreps, width=width),
        out_shape=jax.ShapeDtypeStruct((irreps, depth, n_j * width), BF16),
        grid_spec=pltpu.PrefetchScalarGridSpec(
            num_scalar_prefetch=1,
            grid=(irreps,),
            in_specs=[whole(cycle.shape), whole(c_label.shape), whole(code.shape)],
            out_specs=pl.BlockSpec((1, depth, n_j * width), lambda r, s: (r, 0, 0)),
            scratch_shapes=[
                pltpu.VMEM((depth, n_j * vir_total), BF16),
                pltpu.VMEM((n_j * vir_total, n_j * width), BF16),
            ],
        ),
        compiler_params=pltpu.CompilerParams(vmem_limit_bytes=48 * 2**20),
        cost_estimate=pl.CostEstimate(
            flops=2 * irreps * depth * n_j * vir_total * n_j * width, bytes_accessed=14 * 2**20, transcendentals=0
        ),
    )(scalars, cycle, c_label, code)


def grouped_kernel(scalars, lhs, block, out, rows, total, packed, *, bounds, irreps, halves, window):
    step = pl.program_id(0)
    groups, n_rows, _ = lhs.shape
    n_i, width = groups // halves, block.shape[2]
    spans = []
    for g in range(groups):
        at = bounds + (g % halves) * (irreps + 1) + (step ^ scalars[g // halves])
        low, high = scalars[at], scalars[at + 1]
        base = pl.multiple_of(jnp.minimum(low // 16 * 16, n_rows - window), 16)
        rows[g * window:(g + 1) * window, :] = lhs[g, pl.ds(base, window), :]
        spans.append((low, high, base))
    product = jnp.dot(rows[...], block[0], preferred_element_type=F32)
    for g, (low, high, base) in enumerate(spans):
        piece = product[g * window:(g + 1) * window]
        row = base + lax.broadcasted_iota(jnp.int32, piece.shape, 0)
        spot = (g, pl.ds(base, window), slice(None))
        total[spot] = jnp.where((row >= low) & (row < high), piece, total[spot])

    @pl.when(step == irreps - 1)
    def _():
        n_fold = out.shape[0]
        part = n_rows // n_fold
        for f in range(n_fold):
            for g in range(groups):
                at, lane = g // halves * part, g % halves * width
                packed[at:at + part, lane:lane + width] = total[g, f * part:(f + 1) * part, :]
            values = packed[...]
            most = jnp.maximum(jnp.max(jnp.abs(values), axis=0, keepdims=True), 1e-30)
            scale = jnp.ceil(jnp.log2(most) * 4.0)
            code = jnp.clip(jnp.round(values * (TOP * jnp.exp2(scale * -0.25))), -TOP, TOP)
            code = jnp.concatenate([code, jnp.broadcast_to(scale, (8, scale.shape[1]))])
            out[f] = code.astype(jnp.int32).astype(jnp.int16)


def whole(shape):
    return pl.BlockSpec(shape, lambda r, s: (0,) * len(shape))


def grouped_product(scalars, lhs, block, n_fold, *, bounds, irreps, halves, window):
    groups, n_rows, depth = lhs.shape
    width = block.shape[2]
    n_i = groups // halves
    share = (n_i * n_rows // n_fold, halves * width)
    shape = (n_fold, share[0] + 8, share[1])
    return pl.pallas_call(
        functools.partial(
            grouped_kernel, bounds=bounds, irreps=irreps, halves=halves, window=window
        ),
        out_shape=jax.ShapeDtypeStruct(shape, jnp.int16),
        grid_spec=pltpu.PrefetchScalarGridSpec(
            num_scalar_prefetch=1,
            grid=(irreps,),
            in_specs=[whole(lhs.shape), pl.BlockSpec((1, depth, width), lambda r, s: (r, 0, 0))],
            out_specs=whole(shape),
            scratch_shapes=[
                pltpu.VMEM((groups * window, depth), BF16),
                pltpu.VMEM((groups, n_rows, width), F32),
                pltpu.VMEM(share, F32),
            ],
        ),
        compiler_params=pltpu.CompilerParams(vmem_limit_bytes=48 * 2**20),
        cost_estimate=pl.CostEstimate(
            flops=2 * irreps * groups * window * depth * width, bytes_accessed=13 * 2**20, transcendentals=0
        ),
    )(scalars, lhs, block)


def body(amplitudes, cycle_block, occ_sizes, vir_sizes, window_i, window_occ):
    irreps = occ_sizes.shape[0]
    n_fold, n_pair = lax.axis_size("fold"), lax.axis_size("pair")
    fold, pair = lax.axis_index("fold"), lax.axis_index("pair")
    c_local, occ_total, j_local, vir_total = cycle_block.shape
    n_i, k_local, a_local, _ = amplitudes.shape
    vmax, omax = vir_total // 4, occ_total // 4
    halves = n_pair // n_i
    a_part = a_local // halves

    occ, _, occ_starts = irrep_labels(occ_sizes, occ_total)
    vir, vir_place, starts = irrep_labels(vir_sizes, vir_total)
    to_place = one_hot_rows(vir_place, vmax)
    kappas = omax + 2 - omax % 2
    k_from = jnp.minimum(occ_starts[:irreps] // 2 * 2, occ_total - kappas)
    own_from = jnp.where(occ[:, None] == jnp.arange(irreps)[None, :], k_from[None, :], 0)
    kappa = jnp.arange(occ_total, dtype=jnp.int32) - jnp.sum(own_from, axis=1)
    to_kappa = one_hot_rows(kappa, kappas)
    own_vir = lax.dynamic_slice_in_dim(vir, fold * c_local, c_local)
    k_own = lax.dynamic_slice_in_dim(occ, pair * k_local, k_local)
    i_labels = label_lookup(window_i, occ, occ_total)
    j_labels = label_lookup(lax.dynamic_slice_in_dim(window_occ, pair * j_local, j_local), occ, occ_total)

    x = i_labels[:, None, None] ^ k_own[None, :, None] ^ own_vir[None, None, :]
    masked = jnp.where(x[..., None] == vir, amplitudes, jnp.zeros_like(amplitudes))
    narrow = pick(masked, "ikac,tc->ikat", to_place)
    narrow = narrow.reshape(n_i, k_local, halves, a_part, vmax).transpose(0, 2, 1, 3, 4)
    narrow = narrow.reshape(n_pair, k_local, a_part, vmax)
    narrow = lax.all_to_all(narrow, "pair", split_axis=0, concat_axis=0, tiled=True)
    cycle = cycle_block.transpose(2, 1, 0, 3).reshape(j_local, occ_total * c_local, vir_total)
    narrow, cycle = lax.optimization_barrier((narrow, cycle))
    narrow = narrow.reshape(occ_total, a_part, vmax)

    i_mine = lax.dynamic_index_in_dim(i_labels, pair // halves, keepdims=False)
    a_mine = lax.dynamic_slice_in_dim(vir, fold * a_local + (pair % halves) * a_part, a_part)
    wide = pick(narrow, "kat,tc->akc", to_place)
    x = i_mine ^ occ[None, :, None] ^ a_mine[:, None, None] ^ vir[None, None, :]
    wide = jnp.where(x == 0, wide, jnp.zeros_like(wide))
    short = pick(to_kappa, "qk,akc->aqc", wide)
    short = short.reshape(a_part, kappas, n_fold, c_local).transpose(2, 0, 1, 3)
    short = short.reshape(n_fold, a_part, kappas * c_local)
    short = lax.all_to_all(short, "fold", split_axis=0, concat_axis=0, tiled=True)
    short = short.reshape(n_fold * a_part, kappas * c_local)
    lhs = lax.all_gather(short, "pair", axis=0)

    inside = starts % a_local
    bounds = [starts // a_local * a_part + jnp.clip(inside - h * a_part, 0, a_part) for h in range(halves)]
    scalars = jnp.concatenate(
        [i_labels, own_vir[:1], own_vir[-1:], k_from * c_local, j_labels]
        + bounds
    ).astype(jnp.int32)
    lanes = math.gcd(vir_total, 128)
    c_label = jnp.tile(own_vir.astype(F32)[:, None], (kappas, lanes)).astype(BF16)
    code = jnp.broadcast_to((vir * vmax + vir_place)[:, None], (vir_total, j_local * vmax))
    blocks = class_blocks(scalars, cycle, c_label, code, n_i=n_i, irreps=irreps, width=vmax)

    most = min(vmax, -(-vmax // a_local) * a_part)
    window = min(-(-(most + 15) // 16) * 16, n_fold * a_part)
    coded = grouped_product(
        scalars, lhs, blocks, n_fold, bounds=n_i + irreps + j_local + 2, irreps=irreps, halves=halves, window=window
    )
    coded = lax.all_to_all(coded, "fold", split_axis=0, concat_axis=0, tiled=True).astype(F32)
    shares = coded[:, :-8] * (jnp.exp2(coded[:, -8:-7] * 0.25) / TOP)
    total = jnp.sum(shares, axis=0).astype(BF16).reshape(n_i, a_part, halves, j_local, vmax)
    total = total.transpose(0, 2, 1, 3, 4).reshape(n_i, a_local, j_local, vmax)
    spread_b = pick(total, "iajt,tb->iajb", to_place)
    x = i_labels[:, None, None] ^ own_vir[None, :, None] ^ j_labels[None, None, :]
    return jnp.where(x[..., None] == vir, spread_b, jnp.zeros_like(spread_b))


def solution(mesh):
    placed = (P(None, "pair", "fold", None), P("fold", None, "pair", None), P(), P(), P(), P())
    return jax.shard_map(
        body, mesh=mesh, in_specs=placed, out_specs=P(None, "fold", "pair", None), check_vma=False
    )
```

```python
import functools
import math

import jax
import jax.numpy as jnp
from jax import lax
from jax.experimental import pallas as pl
from jax.experimental.pallas import tpu as pltpu
from jax.sharding import PartitionSpec as P

BF16, F32 = jnp.bfloat16, jnp.float32
TOP = 32767.0


def irrep_labels(sizes, count):
    order = jnp.arange(sizes.shape[1], dtype=jnp.int32)
    positions = jnp.arange(count, dtype=jnp.int32)
    ends = jnp.sum(jnp.where(order[None, None, :] <= order[None, :, None], sizes[:, None, :], 0), axis=2)
    after = positions[None, :, None] >= ends[:, None, :]
    labels = jnp.sum(after.astype(jnp.int32), axis=2)
    places = positions - jnp.sum(jnp.where(after, sizes[:, None, :], 0), axis=2)
    return labels, places, jnp.concatenate([jnp.zeros((sizes.shape[0], 1), jnp.int32), ends], axis=1)


def label_lookup(orbitals, labels, count):
    matches = orbitals[:, None] == jnp.arange(count, dtype=jnp.int32)[None, :]
    return jnp.sum(jnp.where(matches, labels[None, :], 0), axis=1)


def one_hot_rows(places, width):
    return (jnp.arange(width, dtype=jnp.int32)[:, None] == places[None, :]).astype(BF16)


def pick(x, spec, y):
    return jnp.einsum(spec, x, y, preferred_element_type=F32).astype(BF16)


def block_kernel(scalars, cycle, c_label, code, out, chosen, picks, *, n_i, irreps, width):
    step = pl.program_id(0)
    n_j = cycle.shape[0]
    depth, vir_total = c_label.shape[0], cycle.shape[2]
    lane = lax.broadcasted_iota(jnp.int32, (vir_total, n_j * width), 1)
    for j in range(n_j):
        wanted = (step ^ scalars[n_i + 2 + irreps + j]) * width + lane - j * width
        own = (lane >= j * width) & (lane < (j + 1) * width) & (code[...] == wanted)
        picks[j * vir_total:(j + 1) * vir_total, :] = own.astype(F32).astype(BF16)

    def place(h, _):
        first = pl.multiple_of(scalars[n_i + 2 + (step ^ h)], 16)
        label = h.astype(F32).astype(BF16)
        for j in range(n_j):
            for at in range(0, vir_total, c_label.shape[1]):
                lanes = slice(at, at + c_label.shape[1])
                spot = slice(j * vir_total + at, j * vir_total + at + c_label.shape[1])
                chosen[:, spot] = jnp.where(
                    c_label[...] == label, cycle[j, pl.ds(first, depth), lanes], chosen[:, spot]
                )
        return 0

    lax.fori_loop(scalars[n_i], scalars[n_i + 1] + 1, place, 0)
    out[0] = jnp.dot(chosen[...], picks[...], preferred_element_type=F32).astype(BF16)


def class_blocks(scalars, cycle, c_label, code, *, n_i, irreps, width):
    n_j, _, vir_total = cycle.shape
    depth = c_label.shape[0]
    return pl.pallas_call(
        functools.partial(block_kernel, n_i=n_i, irreps=irreps, width=width),
        out_shape=jax.ShapeDtypeStruct((irreps, depth, n_j * width), BF16),
        grid_spec=pltpu.PrefetchScalarGridSpec(
            num_scalar_prefetch=1,
            grid=(irreps,),
            in_specs=[whole(cycle.shape), whole(c_label.shape), whole(code.shape)],
            out_specs=pl.BlockSpec((1, depth, n_j * width), lambda r, s: (r, 0, 0)),
            scratch_shapes=[
                pltpu.VMEM((depth, n_j * vir_total), BF16),
                pltpu.VMEM((n_j * vir_total, n_j * width), BF16),
            ],
        ),
        compiler_params=pltpu.CompilerParams(vmem_limit_bytes=48 * 2**20),
        cost_estimate=pl.CostEstimate(
            flops=2 * irreps * depth * n_j * vir_total * n_j * width, bytes_accessed=14 * 2**20, transcendentals=0
        ),
    )(scalars, cycle, c_label, code)


def grouped_kernel(scalars, lhs, block, out, rows, total, packed, *, bounds, irreps, halves, window):
    step = pl.program_id(0)
    groups, n_rows, _ = lhs.shape
    n_i, width = groups // halves, block.shape[2]
    spans = []
    for g in range(groups):
        at = bounds + (g % halves) * (irreps + 1) + (step ^ scalars[g // halves])
        low, high = scalars[at], scalars[at + 1]
        base = pl.multiple_of(jnp.minimum(low // 16 * 16, n_rows - window), 16)
        rows[g * window:(g + 1) * window, :] = lhs[g, pl.ds(base, window), :]
        spans.append((low, high, base))
    product = jnp.dot(rows[...], block[0], preferred_element_type=F32)
    for g, (low, high, base) in enumerate(spans):
        piece = product[g * window:(g + 1) * window]
        row = base + lax.broadcasted_iota(jnp.int32, piece.shape, 0)
        spot = (g, pl.ds(base, window), slice(None))
        total[spot] = jnp.where((row >= low) & (row < high), piece, total[spot])

    @pl.when(step == irreps - 1)
    def _():
        n_fold = out.shape[0]
        part = n_rows // n_fold
        for f in range(n_fold):
            for g in range(groups):
                at, lane = g // halves * part, g % halves * width
                packed[at:at + part, lane:lane + width] = total[g, f * part:(f + 1) * part, :]
            values = packed[...]
            most = jnp.maximum(jnp.max(jnp.abs(values), axis=0, keepdims=True), 1e-30)
            scale = jnp.ceil(jnp.log2(most) * 4.0)
            code = jnp.clip(jnp.round(values * (TOP * jnp.exp2(scale * -0.25))), -TOP, TOP)
            code = jnp.concatenate([code, jnp.broadcast_to(scale, (8, scale.shape[1]))])
            out[f] = code.astype(jnp.int32).astype(jnp.int16)


def narrow_c_kernel(x, row_label, label, to_place, out, line, *, a_local):
    masked = jnp.where(row_label[0] == label[...], x[0].astype(F32), 0.0).astype(BF16)
    narrow = lax.dot_general(
        to_place[...], masked, (((1,), (1,)), ((), ())), preferred_element_type=F32
    )
    halves, rows = out.shape[0], out.shape[2]
    part = a_local // halves
    for h in range(halves):
        for k in range(rows // part):
            line[:, k * part:(k + 1) * part] = narrow[:, k * a_local + h * part:k * a_local + (h + 1) * part]
        out[h] = line[...].astype(BF16)


def narrow_c(x, row_label, label, to_place, halves, a_local):
    n_i, rows, vir_total = x.shape
    width = to_place.shape[0]
    return pl.pallas_call(
        functools.partial(narrow_c_kernel, a_local=a_local),
        out_shape=jax.ShapeDtypeStruct((n_i * halves, width, rows // halves), BF16),
        grid=(n_i,),
        in_specs=[
            pl.BlockSpec((1, rows, vir_total), lambda i: (i, 0, 0)),
            pl.BlockSpec((1, rows, 1), lambda i: (i, 0, 0)),
            pl.BlockSpec(label.shape, lambda i: (0, 0)),
            pl.BlockSpec(to_place.shape, lambda i: (0, 0)),
        ],
        out_specs=pl.BlockSpec((halves, width, rows // halves), lambda i: (i, 0, 0)),
        scratch_shapes=[pltpu.VMEM((width, rows // halves), F32)],
        compiler_params=pltpu.CompilerParams(vmem_limit_bytes=32 * 2**20),
        cost_estimate=pl.CostEstimate(
            flops=2 * x.size * width, bytes_accessed=3 * 2**20, transcendentals=0
        ),
    )(x, row_label, label, to_place)


def narrow_k_kernel(x, to_place, row_label, label, to_row, out, wide, short, line):
    n_fold, a_part, depth = out.shape
    a_rows = line.shape[0]
    c_local = wide.shape[1] // n_fold
    sources, _, rows = x.shape
    room = wide.shape[0] // sources
    for p in range(sources):
        spread = lax.dot_general(x[p], to_place[...], (((0,), (0,)), ((), ())), preferred_element_type=F32)
        spread = jnp.where(row_label[p] == label[...], spread, 0.0)
        if room > rows:
            spread = jnp.concatenate([spread, jnp.zeros((room - rows, spread.shape[1]), F32)])
        wide[p * room:(p + 1) * room, :] = spread.astype(BF16)
    short[...] = jnp.dot(to_row[...], wide[...], preferred_element_type=F32)
    for f in range(n_fold):
        for q in range(depth // c_local):
            line[:, q * c_local:(q + 1) * c_local] = (
                short[q * a_rows:(q + 1) * a_rows, f * c_local:(f + 1) * c_local]
            )
        out[f] = line[:a_part, :].astype(BF16)


def narrow_k(x, to_place, row_label, label, to_row, n_fold, a_part, c_local):
    vir_total = label.shape[1]
    a_rows = -(-a_part // 8) * 8
    depth = to_row.shape[0] // a_rows * c_local
    return pl.pallas_call(
        narrow_k_kernel,
        out_shape=jax.ShapeDtypeStruct((n_fold, a_part, depth), BF16),
        scratch_shapes=[
            pltpu.VMEM((to_row.shape[1], vir_total), BF16),
            pltpu.VMEM((to_row.shape[0], vir_total), F32),
            pltpu.VMEM((a_rows, depth), F32),
        ],
        compiler_params=pltpu.CompilerParams(vmem_limit_bytes=32 * 2**20),
        cost_estimate=pl.CostEstimate(
            flops=2 * to_row.size * vir_total, bytes_accessed=3 * 2**20, transcendentals=0
        ),
    )(x, to_place, row_label, label, to_row)


def whole(shape):
    return pl.BlockSpec(shape, lambda r, s: (0,) * len(shape))


def grouped_product(scalars, lhs, block, n_fold, *, bounds, irreps, halves, window):
    groups, n_rows, depth = lhs.shape
    width = block.shape[2]
    n_i = groups // halves
    share = (n_i * n_rows // n_fold, halves * width)
    shape = (n_fold, share[0] + 8, share[1])
    return pl.pallas_call(
        functools.partial(
            grouped_kernel, bounds=bounds, irreps=irreps, halves=halves, window=window
        ),
        out_shape=jax.ShapeDtypeStruct(shape, jnp.int16),
        grid_spec=pltpu.PrefetchScalarGridSpec(
            num_scalar_prefetch=1,
            grid=(irreps,),
            in_specs=[whole(lhs.shape), pl.BlockSpec((1, depth, width), lambda r, s: (r, 0, 0))],
            out_specs=whole(shape),
            scratch_shapes=[
                pltpu.VMEM((groups * window, depth), BF16),
                pltpu.VMEM((groups, n_rows, width), F32),
                pltpu.VMEM(share, F32),
            ],
        ),
        compiler_params=pltpu.CompilerParams(vmem_limit_bytes=48 * 2**20),
        cost_estimate=pl.CostEstimate(
            flops=2 * irreps * groups * window * depth * width, bytes_accessed=13 * 2**20, transcendentals=0
        ),
    )(scalars, lhs, block)


def body(amplitudes, cycle_block, occ_sizes, vir_sizes, window_i, window_occ):
    irreps = occ_sizes.shape[0]
    n_fold, n_pair = lax.axis_size("fold"), lax.axis_size("pair")
    fold, pair = lax.axis_index("fold"), lax.axis_index("pair")
    c_local, occ_total, j_local, vir_total = cycle_block.shape
    n_i, k_local, a_local, _ = amplitudes.shape
    vmax, omax = vir_total // 4, occ_total // 4
    halves = n_pair // n_i
    a_part = a_local // halves

    labels, places, all_starts = irrep_labels(jnp.stack([occ_sizes, vir_sizes]), vir_total)
    occ, vir, vir_place = labels[0, :occ_total], labels[1], places[1]
    occ_starts, starts = all_starts[0], all_starts[1]
    to_place = one_hot_rows(vir_place, vmax)
    kappas = omax + 2 - omax % 2
    k_from = jnp.minimum(occ_starts[:irreps] // 2 * 2, occ_total - kappas)
    own_from = jnp.where(occ[:, None] == jnp.arange(irreps)[None, :], k_from[None, :], 0)
    kappa = jnp.arange(occ_total, dtype=jnp.int32) - jnp.sum(own_from, axis=1)
    to_kappa = one_hot_rows(kappa, kappas)
    own_vir = lax.dynamic_slice_in_dim(vir, fold * c_local, c_local)
    k_own = lax.dynamic_slice_in_dim(occ, pair * k_local, k_local)
    i_labels = label_lookup(window_i, occ, occ_total)
    j_labels = label_lookup(lax.dynamic_slice_in_dim(window_occ, pair * j_local, j_local), occ, occ_total)

    x = (i_labels[:, None, None] ^ k_own[None, :, None] ^ own_vir[None, None, :]).reshape(n_i, -1, 1)
    narrow = narrow_c(amplitudes.reshape(n_i, -1, vir_total), x, vir[None, :], to_place, halves, a_local)
    narrow = lax.all_to_all(narrow, "pair", split_axis=0, concat_axis=0, tiled=True)
    cycle = cycle_block.transpose(2, 1, 0, 3).reshape(j_local, occ_total * c_local, vir_total)
    narrow, cycle = lax.optimization_barrier((narrow, cycle))

    i_mine = lax.dynamic_index_in_dim(i_labels, pair // halves, keepdims=False)
    a_mine = lax.dynamic_slice_in_dim(vir, fold * a_local + (pair % halves) * a_part, a_part)
    x = (i_mine ^ occ[:, None] ^ a_mine[None, :]).reshape(n_pair, k_local * a_part, 1)
    a_rows = -(-a_part // 8) * 8
    room = -(-k_local * a_part // 16) * 16
    row = jnp.arange(kappas * a_rows, dtype=jnp.int32)[:, None]
    k_kappa = jnp.repeat(kappa, a_part).reshape(n_pair, -1)
    k_kappa = jnp.pad(k_kappa, ((0, 0), (0, room - k_kappa.shape[1])), constant_values=-1).reshape(1, -1)
    column = jnp.arange(n_pair * room, dtype=jnp.int32)[None, :] % room % a_part
    to_row = ((row // a_rows == k_kappa) & (row % a_rows == column)).astype(BF16)
    short = narrow_k(narrow, to_place, x, vir[None, :], to_row, n_fold, a_part, c_local)
    short = lax.all_to_all(short, "fold", split_axis=0, concat_axis=0, tiled=True)
    short = short.reshape(n_fold * a_part, kappas * c_local)
    lhs = lax.all_gather(short, "pair", axis=0)

    inside = starts % a_local
    bounds = [starts // a_local * a_part + jnp.clip(inside - h * a_part, 0, a_part) for h in range(halves)]
    scalars = jnp.concatenate(
        [i_labels, own_vir[:1], own_vir[-1:], k_from * c_local, j_labels]
        + bounds
    ).astype(jnp.int32)
    lanes = math.gcd(vir_total, 128)
    c_label = jnp.tile(own_vir.astype(F32)[:, None], (kappas, lanes)).astype(BF16)
    code = jnp.broadcast_to((vir * vmax + vir_place)[:, None], (vir_total, j_local * vmax))
    blocks = class_blocks(scalars, cycle, c_label, code, n_i=n_i, irreps=irreps, width=vmax)

    most = min(vmax, -(-vmax // a_local) * a_part)
    window = min(-(-(most + 15) // 16) * 16, n_fold * a_part)
    coded = grouped_product(
        scalars, lhs, blocks, n_fold, bounds=n_i + irreps + j_local + 2, irreps=irreps, halves=halves, window=window
    )
    coded = lax.all_to_all(coded, "fold", split_axis=0, concat_axis=0, tiled=True).astype(F32)
    shares = coded[:, :-8] * (jnp.exp2(coded[:, -8:-7] * 0.25) / TOP)
    total = jnp.sum(shares, axis=0).astype(BF16).reshape(n_i, a_part, halves, j_local, vmax)
    total = total.transpose(0, 2, 1, 3, 4).reshape(n_i, a_local, j_local, vmax)
    spread_b = pick(total, "iajt,tb->iajb", to_place)
    x = i_labels[:, None, None] ^ own_vir[None, :, None] ^ j_labels[None, None, :]
    return jnp.where(x[..., None] == vir, spread_b, jnp.zeros_like(spread_b))


def solution(mesh):
    placed = (P(None, "pair", "fold", None), P("fold", None, "pair", None), P(), P(), P(), P())
    return jax.shard_map(
        body, mesh=mesh, in_specs=placed, out_specs=P(None, "fold", "pair", None), check_vma=False
    )
```

```python
import functools
import math

import jax
import jax.numpy as jnp
from jax import lax
from jax.experimental import pallas as pl
from jax.experimental.pallas import tpu as pltpu
from jax.sharding import PartitionSpec as P

BF16, F32 = jnp.bfloat16, jnp.float32
TOP = 32767.0


def irrep_labels(sizes, count):
    order = jnp.arange(sizes.shape[1], dtype=jnp.int32)
    positions = jnp.arange(count, dtype=jnp.int32)
    ends = jnp.sum(jnp.where(order[None, None, :] <= order[None, :, None], sizes[:, None, :], 0), axis=2)
    after = positions[None, :, None] >= ends[:, None, :]
    labels = jnp.sum(after.astype(jnp.int32), axis=2)
    places = positions - jnp.sum(jnp.where(after, sizes[:, None, :], 0), axis=2)
    return labels, places, jnp.concatenate([jnp.zeros((sizes.shape[0], 1), jnp.int32), ends], axis=1)


def label_lookup(orbitals, labels, count):
    matches = orbitals[:, None] == jnp.arange(count, dtype=jnp.int32)[None, :]
    return jnp.sum(jnp.where(matches, labels[None, :], 0), axis=1)


def one_hot_rows(places, width):
    return (jnp.arange(width, dtype=jnp.int32)[:, None] == places[None, :]).astype(BF16)


def pick(x, spec, y):
    return jnp.einsum(spec, x, y, preferred_element_type=F32).astype(BF16)


def tile_spans(c_local):
    spans = []
    for first in range(0, 2 * c_local, 16):
        runs = []
        for row in range(first, first + 16):
            c = row % c_local
            if runs and c == runs[-1][1] + 1:
                runs[-1][1] = c
            else:
                runs.append([c, c])
        spans.append(runs)
    return spans


def block_kernel(scalars, cycle, c_label, picks, out, chosen, *, n_i, irreps, owns):
    step = pl.program_id(0)
    n_j, _, pair_rows, vir_total = cycle.shape
    k_pairs, width = chosen.shape[1], picks.shape[2]
    for tile, runs in enumerate(tile_spans(pair_rows // 2)):
        rows = slice(16 * tile, 16 * tile + 16)

        def place(h, _):
            first = scalars[n_i + (step ^ h)]
            own = c_label[rows, :] == h.astype(F32).astype(BF16)
            own = jnp.broadcast_to(own[None], (k_pairs,) + own.shape)
            for j in range(n_j):
                chosen[j, :, rows, :] = jnp.where(
                    own, cycle[j, pl.ds(first, k_pairs), rows, :], chosen[j, :, rows, :]
                )
            return 0

        for low, high in runs:
            lax.fori_loop(scalars[owns + low], scalars[owns + high] + 1, place, 0)
    for j in range(n_j):
        narrow = jnp.dot(
            chosen[j].reshape(k_pairs * pair_rows, vir_total),
            picks[step ^ scalars[n_i + irreps + j]],
            preferred_element_type=F32,
        )
        out[0, :, j * width:(j + 1) * width] = narrow.astype(BF16)


def class_blocks(scalars, cycle, c_label, picks, *, n_i, irreps, owns, k_pairs):
    n_j, _, pair_rows, vir_total = cycle.shape
    width = picks.shape[2]
    depth = k_pairs * pair_rows
    return pl.pallas_call(
        functools.partial(block_kernel, n_i=n_i, irreps=irreps, owns=owns),
        out_shape=jax.ShapeDtypeStruct((irreps, depth, n_j * width), BF16),
        grid_spec=pltpu.PrefetchScalarGridSpec(
            num_scalar_prefetch=1,
            grid=(irreps,),
            in_specs=[whole(cycle.shape), whole(c_label.shape), whole(picks.shape)],
            out_specs=pl.BlockSpec((1, depth, n_j * width), lambda r, s: (r, 0, 0)),
            scratch_shapes=[pltpu.VMEM((n_j, k_pairs, pair_rows, vir_total), BF16)],
        ),
        compiler_params=pltpu.CompilerParams(vmem_limit_bytes=48 * 2**20),
        cost_estimate=pl.CostEstimate(
            flops=2 * irreps * depth * n_j * vir_total * width, bytes_accessed=14 * 2**20, transcendentals=0
        ),
    )(scalars, cycle, c_label, picks)


def grouped_kernel(scalars, lhs, block, out, rows, total, packed, *, bounds, irreps, halves, window):
    step = pl.program_id(0)
    groups, n_rows, _ = lhs.shape
    n_i, width = groups // halves, block.shape[2]
    spans = []
    for g in range(groups):
        at = bounds + (g % halves) * (irreps + 1) + (step ^ scalars[g // halves])
        low, high = scalars[at], scalars[at + 1]
        base = pl.multiple_of(jnp.minimum(low // 16 * 16, n_rows - window), 16)
        rows[g * window:(g + 1) * window, :] = lhs[g, pl.ds(base, window), :]
        spans.append((low, high, base))
    product = jnp.dot(rows[...], block[0], preferred_element_type=F32)
    for g, (low, high, base) in enumerate(spans):
        piece = product[g * window:(g + 1) * window]
        row = base + lax.broadcasted_iota(jnp.int32, piece.shape, 0)
        spot = (g, pl.ds(base, window), slice(None))
        total[spot] = jnp.where((row >= low) & (row < high), piece, total[spot])

    @pl.when(step == irreps - 1)
    def _():
        n_fold = out.shape[0]
        part = n_rows // n_fold
        for f in range(n_fold):
            for g in range(groups):
                at, lane = g // halves * part, g % halves * width
                packed[at:at + part, lane:lane + width] = total[g, f * part:(f + 1) * part, :]
            values = packed[...]
            most = jnp.maximum(jnp.max(jnp.abs(values), axis=0, keepdims=True), 1e-30)
            scale = jnp.ceil(jnp.log2(most) * 4.0)
            code = jnp.clip(jnp.round(values * (TOP * jnp.exp2(scale * -0.25))), -TOP, TOP)
            code = jnp.concatenate([code, jnp.broadcast_to(scale, (8, scale.shape[1]))])
            out[f] = code.astype(jnp.int32).astype(jnp.int16)


def narrow_c_kernel(scalars, x, a_label, label, to_place, out, masked, line, *, n_i, a_local):
    i_label = scalars[pl.program_id(0)]
    between = a_label[...] ^ label[...]
    for k in range(masked.shape[0] // a_local):
        rows = slice(k * a_local, (k + 1) * a_local)
        own = between == (i_label ^ scalars[n_i + k])
        masked[rows, :] = jnp.where(own, x[0, k].astype(F32), 0.0)
    narrow = lax.dot_general(
        to_place[...], masked[...].astype(BF16), (((1,), (1,)), ((), ())), preferred_element_type=F32
    )
    halves, rows = out.shape[0], out.shape[2]
    part = a_local // halves
    for h in range(halves):
        for k in range(rows // part):
            line[:, k * part:(k + 1) * part] = narrow[:, k * a_local + h * part:k * a_local + (h + 1) * part]
        out[h] = line[...].astype(BF16)


def narrow_c(scalars, x, a_label, label, to_place, halves):
    n_i, k_local, a_local, vir_total = x.shape
    width = to_place.shape[0]
    rows = k_local * a_local
    return pl.pallas_call(
        functools.partial(narrow_c_kernel, n_i=n_i, a_local=a_local),
        out_shape=jax.ShapeDtypeStruct((n_i * halves, width, rows // halves), BF16),
        grid_spec=pltpu.PrefetchScalarGridSpec(
            num_scalar_prefetch=1,
            grid=(n_i,),
            in_specs=[
                pl.BlockSpec((1, k_local, a_local, vir_total), lambda i, s: (i, 0, 0, 0)),
                whole(a_label.shape),
                whole(label.shape),
                whole(to_place.shape),
            ],
            out_specs=pl.BlockSpec((halves, width, rows // halves), lambda i, s: (i, 0, 0)),
            scratch_shapes=[pltpu.VMEM((rows, vir_total), F32), pltpu.VMEM((width, rows // halves), F32)],
        ),
        compiler_params=pltpu.CompilerParams(vmem_limit_bytes=32 * 2**20),
        cost_estimate=pl.CostEstimate(
            flops=2 * x.size * width, bytes_accessed=3 * 2**20, transcendentals=0
        ),
    )(scalars, x, a_label, label, to_place)


def narrow_k_kernel(x, to_place, row_label, label, to_row, out, wide, short, line):
    n_fold, a_part, depth = out.shape
    a_rows = line.shape[0]
    c_local = wide.shape[1] // n_fold
    sources, _, rows = x.shape
    room = wide.shape[0] // sources
    for p in range(sources):
        spread = lax.dot_general(x[p], to_place[...], (((0,), (0,)), ((), ())), preferred_element_type=F32)
        spread = jnp.where(row_label[p] == label[...], spread, 0.0)
        if room > rows:
            spread = jnp.concatenate([spread, jnp.zeros((room - rows, spread.shape[1]), F32)])
        wide[p * room:(p + 1) * room, :] = spread.astype(BF16)
    short[...] = jnp.dot(to_row[...], wide[...], preferred_element_type=F32)
    for f in range(n_fold):
        for q in range(depth // c_local):
            line[:, q * c_local:(q + 1) * c_local] = (
                short[q * a_rows:(q + 1) * a_rows, f * c_local:(f + 1) * c_local]
            )
        out[f] = line[:a_part, :].astype(BF16)


def narrow_k(x, to_place, row_label, label, to_row, n_fold, a_part, c_local):
    vir_total = label.shape[1]
    a_rows = -(-a_part // 8) * 8
    depth = to_row.shape[0] // a_rows * c_local
    return pl.pallas_call(
        narrow_k_kernel,
        out_shape=jax.ShapeDtypeStruct((n_fold, a_part, depth), BF16),
        scratch_shapes=[
            pltpu.VMEM((to_row.shape[1], vir_total), BF16),
            pltpu.VMEM((to_row.shape[0], vir_total), F32),
            pltpu.VMEM((a_rows, depth), F32),
        ],
        compiler_params=pltpu.CompilerParams(vmem_limit_bytes=32 * 2**20),
        cost_estimate=pl.CostEstimate(
            flops=2 * to_row.size * vir_total, bytes_accessed=3 * 2**20, transcendentals=0
        ),
    )(x, to_place, row_label, label, to_row)


def whole(shape):
    return pl.BlockSpec(shape, lambda r, s: (0,) * len(shape))


def grouped_product(scalars, lhs, block, n_fold, *, bounds, irreps, halves, window):
    groups, n_rows, depth = lhs.shape
    width = block.shape[2]
    n_i = groups // halves
    share = (n_i * n_rows // n_fold, halves * width)
    shape = (n_fold, share[0] + 8, share[1])
    return pl.pallas_call(
        functools.partial(
            grouped_kernel, bounds=bounds, irreps=irreps, halves=halves, window=window
        ),
        out_shape=jax.ShapeDtypeStruct(shape, jnp.int16),
        grid_spec=pltpu.PrefetchScalarGridSpec(
            num_scalar_prefetch=1,
            grid=(irreps,),
            in_specs=[whole(lhs.shape), pl.BlockSpec((1, depth, width), lambda r, s: (r, 0, 0))],
            out_specs=whole(shape),
            scratch_shapes=[
                pltpu.VMEM((groups * window, depth), BF16),
                pltpu.VMEM((groups, n_rows, width), F32),
                pltpu.VMEM(share, F32),
            ],
        ),
        compiler_params=pltpu.CompilerParams(vmem_limit_bytes=48 * 2**20),
        cost_estimate=pl.CostEstimate(
            flops=2 * irreps * groups * window * depth * width, bytes_accessed=13 * 2**20, transcendentals=0
        ),
    )(scalars, lhs, block)


def body(amplitudes, cycle_block, occ_sizes, vir_sizes, window_i, window_occ):
    irreps = occ_sizes.shape[0]
    n_fold, n_pair = lax.axis_size("fold"), lax.axis_size("pair")
    fold, pair = lax.axis_index("fold"), lax.axis_index("pair")
    c_local, occ_total, j_local, vir_total = cycle_block.shape
    n_i, k_local, a_local, _ = amplitudes.shape
    vmax, omax = vir_total // 4, occ_total // 4
    halves = n_pair // n_i
    a_part = a_local // halves

    labels, places, all_starts = irrep_labels(jnp.stack([occ_sizes, vir_sizes]), vir_total)
    occ, vir, vir_place = labels[0, :occ_total], labels[1], places[1]
    occ_starts, starts = all_starts[0], all_starts[1]
    to_place = one_hot_rows(vir_place, vmax)
    kappas = omax + 2 - omax % 2
    k_from = jnp.minimum(occ_starts[:irreps] // 2 * 2, occ_total - kappas)
    own_from = jnp.where(occ[:, None] == jnp.arange(irreps)[None, :], k_from[None, :], 0)
    kappa = jnp.arange(occ_total, dtype=jnp.int32) - jnp.sum(own_from, axis=1)
    to_kappa = one_hot_rows(kappa, kappas)
    own_vir = lax.dynamic_slice_in_dim(vir, fold * c_local, c_local)
    k_own = lax.dynamic_slice_in_dim(occ, pair * k_local, k_local)
    i_labels = label_lookup(window_i, occ, occ_total)
    j_labels = label_lookup(lax.dynamic_slice_in_dim(window_occ, pair * j_local, j_local), occ, occ_total)

    narrow = narrow_c(
        jnp.concatenate([i_labels, k_own]), amplitudes, own_vir[:, None], vir[None, :], to_place, halves
    )
    narrow = lax.all_to_all(narrow, "pair", split_axis=0, concat_axis=0, tiled=True)
    cycle = cycle_block.transpose(2, 1, 0, 3).reshape(j_local, occ_total // 2, 2 * c_local, vir_total)
    code = (vir * vmax + vir_place)[None, :, None]
    spots = jnp.arange(irreps * vmax, dtype=jnp.int32).reshape(irreps, 1, vmax)
    picks = (code == spots).astype(BF16)
    narrow, cycle, picks = lax.optimization_barrier((narrow, cycle, picks))

    i_mine = lax.dynamic_index_in_dim(i_labels, pair // halves, keepdims=False)
    a_mine = lax.dynamic_slice_in_dim(vir, fold * a_local + (pair % halves) * a_part, a_part)
    x = (i_mine ^ occ[:, None] ^ a_mine[None, :]).reshape(n_pair, k_local * a_part, 1)
    a_rows = -(-a_part // 8) * 8
    room = -(-k_local * a_part // 16) * 16
    row = jnp.arange(kappas * a_rows, dtype=jnp.int32)[:, None]
    k_kappa = jnp.repeat(kappa, a_part).reshape(n_pair, -1)
    k_kappa = jnp.pad(k_kappa, ((0, 0), (0, room - k_kappa.shape[1])), constant_values=-1).reshape(1, -1)
    column = jnp.arange(n_pair * room, dtype=jnp.int32)[None, :] % room % a_part
    to_row = ((row // a_rows == k_kappa) & (row % a_rows == column)).astype(BF16)
    short = narrow_k(narrow, to_place, x, vir[None, :], to_row, n_fold, a_part, c_local)
    short = lax.all_to_all(short, "fold", split_axis=0, concat_axis=0, tiled=True)
    short = short.reshape(n_fold * a_part, kappas * c_local)
    lhs = lax.all_gather(short, "pair", axis=0)

    inside = starts % a_local
    bounds = [starts // a_local * a_part + jnp.clip(inside - h * a_part, 0, a_part) for h in range(halves)]
    scalars = jnp.concatenate([i_labels, k_from // 2, j_labels] + bounds + [own_vir]).astype(jnp.int32)
    low = n_i + irreps + j_local
    c_label = jnp.broadcast_to(jnp.tile(own_vir.astype(F32), 2)[:, None], (2 * c_local, vir_total)).astype(BF16)
    blocks = class_blocks(
        scalars, cycle, c_label, picks, n_i=n_i, irreps=irreps, owns=low + halves * (irreps + 1), k_pairs=kappas // 2
    )

    most = min(vmax, -(-vmax // a_local) * a_part)
    window = min(-(-(most + 15) // 16) * 16, n_fold * a_part)
    coded = grouped_product(
        scalars, lhs, blocks, n_fold, bounds=low, irreps=irreps, halves=halves, window=window
    )
    coded = lax.all_to_all(coded, "fold", split_axis=0, concat_axis=0, tiled=True).astype(F32)
    shares = coded[:, :-8] * (jnp.exp2(coded[:, -8:-7] * 0.25) / TOP)
    total = jnp.sum(shares, axis=0).astype(BF16).reshape(n_i, a_part, halves, j_local, vmax)
    total = total.transpose(0, 2, 1, 3, 4).reshape(n_i, a_local, j_local, vmax)
    spread_b = pick(total, "iajt,tb->iajb", to_place)
    x = i_labels[:, None, None] ^ own_vir[None, :, None] ^ j_labels[None, None, :]
    return jnp.where(x[..., None] == vir, spread_b, jnp.zeros_like(spread_b))


def solution(mesh):
    placed = (P(None, "pair", "fold", None), P("fold", None, "pair", None), P(), P(), P(), P())
    return jax.shard_map(
        body, mesh=mesh, in_specs=placed, out_specs=P(None, "fold", "pair", None), check_vma=False
    )
```

```python
import functools
import math

import jax
import jax.numpy as jnp
from jax import lax
from jax.experimental import pallas as pl
from jax.experimental.pallas import tpu as pltpu
from jax.sharding import PartitionSpec as P

BF16, F32 = jnp.bfloat16, jnp.float32
TOP = 32767.0


def irrep_labels(sizes, count):
    order = jnp.arange(sizes.shape[1], dtype=jnp.int32)
    positions = jnp.arange(count, dtype=jnp.int32)
    ends = jnp.sum(jnp.where(order[None, None, :] <= order[None, :, None], sizes[:, None, :], 0), axis=2)
    after = positions[None, :, None] >= ends[:, None, :]
    labels = jnp.sum(after.astype(jnp.int32), axis=2)
    places = positions - jnp.sum(jnp.where(after, sizes[:, None, :], 0), axis=2)
    return labels, places, jnp.concatenate([jnp.zeros((sizes.shape[0], 1), jnp.int32), ends], axis=1)


def label_lookup(orbitals, labels, count):
    matches = orbitals[:, None] == jnp.arange(count, dtype=jnp.int32)[None, :]
    return jnp.sum(jnp.where(matches, labels[None, :], 0), axis=1)


def one_hot_rows(places, width):
    return (jnp.arange(width, dtype=jnp.int32)[:, None] == places[None, :]).astype(BF16)


def pick(x, spec, y):
    return jnp.einsum(spec, x, y, preferred_element_type=F32).astype(BF16)


def tile_spans(c_local):
    spans = []
    for first in range(0, 2 * c_local, 16):
        runs = []
        for row in range(first, first + 16):
            c = row % c_local
            if runs and c == runs[-1][1] + 1:
                runs[-1][1] = c
            else:
                runs.append([c, c])
        spans.append(runs)
    return spans


def block_kernel(scalars, cycle, c_label, picks, out, chosen, *, n_i, irreps, owns):
    step = pl.program_id(0)
    n_j, _, pair_rows, vir_total = cycle.shape
    k_pairs, width = chosen.shape[1], picks.shape[2]
    for tile, runs in enumerate(tile_spans(pair_rows // 2)):
        rows = slice(16 * tile, 16 * tile + 16)

        def place(h, _):
            first = scalars[n_i + (step ^ h)]
            own = c_label[rows, :] == h.astype(F32).astype(BF16)
            own = jnp.broadcast_to(own[None], (k_pairs,) + own.shape)
            for j in range(n_j):
                chosen[j, :, rows, :] = jnp.where(
                    own, cycle[j, pl.ds(first, k_pairs), rows, :], chosen[j, :, rows, :]
                )
            return 0

        for low, high in runs:
            lax.fori_loop(scalars[owns + low], scalars[owns + high] + 1, place, 0)
    for j in range(n_j):
        narrow = jnp.dot(
            chosen[j].reshape(k_pairs * pair_rows, vir_total),
            picks[step ^ scalars[n_i + irreps + j]],
            preferred_element_type=F32,
        )
        out[0, :, j * width:(j + 1) * width] = narrow.astype(BF16)


def class_blocks(scalars, cycle, c_label, picks, *, n_i, irreps, owns, k_pairs):
    n_j, _, pair_rows, vir_total = cycle.shape
    width = picks.shape[2]
    depth = k_pairs * pair_rows
    return pl.pallas_call(
        functools.partial(block_kernel, n_i=n_i, irreps=irreps, owns=owns),
        out_shape=jax.ShapeDtypeStruct((irreps, depth, n_j * width), BF16),
        grid_spec=pltpu.PrefetchScalarGridSpec(
            num_scalar_prefetch=1,
            grid=(irreps,),
            in_specs=[whole(cycle.shape), whole(c_label.shape), whole(picks.shape)],
            out_specs=pl.BlockSpec((1, depth, n_j * width), lambda r, s: (r, 0, 0)),
            scratch_shapes=[pltpu.VMEM((n_j, k_pairs, pair_rows, vir_total), BF16)],
        ),
        compiler_params=pltpu.CompilerParams(vmem_limit_bytes=48 * 2**20),
        cost_estimate=pl.CostEstimate(
            flops=2 * irreps * depth * n_j * vir_total * width, bytes_accessed=14 * 2**20, transcendentals=0
        ),
    )(scalars, cycle, c_label, picks)


def gather_pieces(v, n_pair):
    def send(value, step):
        return lax.ppermute(value, "pair", [(p, (p + step) % n_pair) for p in range(n_pair)])

    half = v.shape[0] // 2
    up, down = send(v, 2), send(v, -2)
    far_up, far_down = send(up[:half], 2), send(down[half:], -2)
    pieces = [v, up, down, far_up, far_down]
    return pieces + [lax.ppermute(p, "pair", [(q, q ^ 1) for q in range(n_pair)]) for p in pieces]


def grouped_kernel(scalars, *refs, bounds, irreps, halves, window, me):
    pieces, (block, out, lhs, rows, total, packed, sems) = refs[:10], refs[10:]
    step = pl.program_id(0)

    @pl.when(step == 0)
    def _():
        y, core = scalars[me] // 2, scalars[me] % 2
        half = lhs.shape[1] // 2
        copies = []
        for n, piece in enumerate(pieces):
            away = (0, -1, 1, 2, 2)[n % 5]
            first = half if n % 5 == 4 else 0
            g = lax.rem(y + away + 4, 4) * 2 + (core if n < 5 else 1 - core)
            copies.append(pltpu.make_async_copy(piece, lhs.at[g, pl.ds(first, piece.shape[0]), :], sems.at[n]))
            copies[-1].start()
        for copy in copies:
            copy.wait()

    groups, n_rows, _ = lhs.shape
    n_i, width = groups // halves, block.shape[2]
    spans = []
    for g in range(groups):
        at = bounds + (g % halves) * (irreps + 1) + (step ^ scalars[g // halves])
        low, high = scalars[at], scalars[at + 1]
        base = pl.multiple_of(jnp.minimum(low // 16 * 16, n_rows - window), 16)
        rows[g * window:(g + 1) * window, :] = lhs[g, pl.ds(base, window), :]
        spans.append((low, high, base))
    product = jnp.dot(rows[...], block[0], preferred_element_type=F32)
    for g, (low, high, base) in enumerate(spans):
        piece = product[g * window:(g + 1) * window]
        row = base + lax.broadcasted_iota(jnp.int32, piece.shape, 0)
        spot = (g, pl.ds(base, window), slice(None))
        total[spot] = jnp.where((row >= low) & (row < high), piece, total[spot])

    @pl.when(step == irreps - 1)
    def _():
        n_fold = out.shape[0]
        part = n_rows // n_fold
        for f in range(n_fold):
            for g in range(groups):
                at, lane = g // halves * part, g % halves * width
                packed[at:at + part, lane:lane + width] = total[g, f * part:(f + 1) * part, :]
            values = packed[...]
            most = jnp.maximum(jnp.max(jnp.abs(values), axis=0, keepdims=True), 1e-30)
            scale = jnp.ceil(jnp.log2(most) * 4.0)
            code = jnp.clip(jnp.round(values * (TOP * jnp.exp2(scale * -0.25))), -TOP, TOP)
            code = jnp.concatenate([code, jnp.broadcast_to(scale, (8, scale.shape[1]))])
            out[f] = code.astype(jnp.int32).astype(jnp.int16)


def narrow_c_kernel(scalars, x, a_label, label, to_place, out, masked, line, *, n_i, a_local):
    i_label = scalars[pl.program_id(0)]
    between = a_label[...] ^ label[...]
    for k in range(masked.shape[0] // a_local):
        rows = slice(k * a_local, (k + 1) * a_local)
        own = between == (i_label ^ scalars[n_i + k])
        masked[rows, :] = jnp.where(own, x[0, k].astype(F32), 0.0)
    narrow = lax.dot_general(
        to_place[...], masked[...].astype(BF16), (((1,), (1,)), ((), ())), preferred_element_type=F32
    )
    halves, rows = out.shape[0], out.shape[2]
    part = a_local // halves
    for h in range(halves):
        for k in range(rows // part):
            line[:, k * part:(k + 1) * part] = narrow[:, k * a_local + h * part:k * a_local + (h + 1) * part]
        out[h] = line[...].astype(BF16)


def narrow_c(scalars, x, a_label, label, to_place, halves):
    n_i, k_local, a_local, vir_total = x.shape
    width = to_place.shape[0]
    rows = k_local * a_local
    return pl.pallas_call(
        functools.partial(narrow_c_kernel, n_i=n_i, a_local=a_local),
        out_shape=jax.ShapeDtypeStruct((n_i * halves, width, rows // halves), BF16),
        grid_spec=pltpu.PrefetchScalarGridSpec(
            num_scalar_prefetch=1,
            grid=(n_i,),
            in_specs=[
                pl.BlockSpec((1, k_local, a_local, vir_total), lambda i, s: (i, 0, 0, 0)),
                whole(a_label.shape),
                whole(label.shape),
                whole(to_place.shape),
            ],
            out_specs=pl.BlockSpec((halves, width, rows // halves), lambda i, s: (i, 0, 0)),
            scratch_shapes=[pltpu.VMEM((rows, vir_total), F32), pltpu.VMEM((width, rows // halves), F32)],
        ),
        compiler_params=pltpu.CompilerParams(vmem_limit_bytes=32 * 2**20),
        cost_estimate=pl.CostEstimate(
            flops=2 * x.size * width, bytes_accessed=3 * 2**20, transcendentals=0
        ),
    )(scalars, x, a_label, label, to_place)


def narrow_k_kernel(x, to_place, row_label, label, to_row, out, wide, short, line):
    n_fold, a_part, depth = out.shape
    a_rows = line.shape[0]
    c_local = wide.shape[1] // n_fold
    sources, _, rows = x.shape
    room = wide.shape[0] // sources
    for p in range(sources):
        spread = lax.dot_general(x[p], to_place[...], (((0,), (0,)), ((), ())), preferred_element_type=F32)
        spread = jnp.where(row_label[p] == label[...], spread, 0.0)
        if room > rows:
            spread = jnp.concatenate([spread, jnp.zeros((room - rows, spread.shape[1]), F32)])
        wide[p * room:(p + 1) * room, :] = spread.astype(BF16)
    short[...] = jnp.dot(to_row[...], wide[...], preferred_element_type=F32)
    for f in range(n_fold):
        for q in range(depth // c_local):
            line[:, q * c_local:(q + 1) * c_local] = (
                short[q * a_rows:(q + 1) * a_rows, f * c_local:(f + 1) * c_local]
            )
        out[f] = line[:a_part, :].astype(BF16)


def narrow_k(x, to_place, row_label, label, to_row, n_fold, a_part, c_local):
    vir_total = label.shape[1]
    a_rows = -(-a_part // 8) * 8
    depth = to_row.shape[0] // a_rows * c_local
    return pl.pallas_call(
        narrow_k_kernel,
        out_shape=jax.ShapeDtypeStruct((n_fold, a_part, depth), BF16),
        scratch_shapes=[
            pltpu.VMEM((to_row.shape[1], vir_total), BF16),
            pltpu.VMEM((to_row.shape[0], vir_total), F32),
            pltpu.VMEM((a_rows, depth), F32),
        ],
        compiler_params=pltpu.CompilerParams(vmem_limit_bytes=32 * 2**20),
        cost_estimate=pl.CostEstimate(
            flops=2 * to_row.size * vir_total, bytes_accessed=3 * 2**20, transcendentals=0
        ),
    )(x, to_place, row_label, label, to_row)


def whole(shape):
    return pl.BlockSpec(shape, lambda r, s: (0,) * len(shape))


def grouped_product(scalars, pieces, block, n_fold, groups, *, bounds, irreps, halves, window, me):
    n_rows, depth = pieces[0].shape
    width = block.shape[2]
    n_i = groups // halves
    share = (n_i * n_rows // n_fold, halves * width)
    shape = (n_fold, share[0] + 8, share[1])
    return pl.pallas_call(
        functools.partial(
            grouped_kernel, bounds=bounds, irreps=irreps, halves=halves, window=window, me=me
        ),
        out_shape=jax.ShapeDtypeStruct(shape, jnp.int16),
        grid_spec=pltpu.PrefetchScalarGridSpec(
            num_scalar_prefetch=1,
            grid=(irreps,),
            in_specs=[pl.BlockSpec(memory_space=pl.ANY)] * len(pieces)
            + [pl.BlockSpec((1, depth, width), lambda r, s: (r, 0, 0))],
            out_specs=whole(shape),
            scratch_shapes=[
                pltpu.VMEM((groups, n_rows, depth), BF16),
                pltpu.VMEM((groups * window, depth), BF16),
                pltpu.VMEM((groups, n_rows, width), F32),
                pltpu.VMEM(share, F32),
                pltpu.SemaphoreType.DMA((len(pieces),)),
            ],
        ),
        compiler_params=pltpu.CompilerParams(vmem_limit_bytes=48 * 2**20),
        cost_estimate=pl.CostEstimate(
            flops=2 * irreps * groups * window * depth * width, bytes_accessed=13 * 2**20, transcendentals=0
        ),
    )(scalars, *pieces, block)


def body(amplitudes, cycle_block, occ_sizes, vir_sizes, window_i, window_occ):
    irreps = occ_sizes.shape[0]
    n_fold, n_pair = lax.axis_size("fold"), lax.axis_size("pair")
    fold, pair = lax.axis_index("fold"), lax.axis_index("pair")
    c_local, occ_total, j_local, vir_total = cycle_block.shape
    n_i, k_local, a_local, _ = amplitudes.shape
    vmax, omax = vir_total // 4, occ_total // 4
    halves = n_pair // n_i
    a_part = a_local // halves

    labels, places, all_starts = irrep_labels(jnp.stack([occ_sizes, vir_sizes]), vir_total)
    occ, vir, vir_place = labels[0, :occ_total], labels[1], places[1]
    occ_starts, starts = all_starts[0], all_starts[1]
    to_place = one_hot_rows(vir_place, vmax)
    kappas = omax + 2 - omax % 2
    k_from = jnp.minimum(occ_starts[:irreps] // 2 * 2, occ_total - kappas)
    own_from = jnp.where(occ[:, None] == jnp.arange(irreps)[None, :], k_from[None, :], 0)
    kappa = jnp.arange(occ_total, dtype=jnp.int32) - jnp.sum(own_from, axis=1)
    to_kappa = one_hot_rows(kappa, kappas)
    own_vir = lax.dynamic_slice_in_dim(vir, fold * c_local, c_local)
    k_own = lax.dynamic_slice_in_dim(occ, pair * k_local, k_local)
    i_labels = label_lookup(window_i, occ, occ_total)
    j_labels = label_lookup(lax.dynamic_slice_in_dim(window_occ, pair * j_local, j_local), occ, occ_total)

    narrow = narrow_c(
        jnp.concatenate([i_labels, k_own]), amplitudes, own_vir[:, None], vir[None, :], to_place, halves
    )
    narrow = lax.all_to_all(narrow, "pair", split_axis=0, concat_axis=0, tiled=True)
    cycle = cycle_block.transpose(2, 1, 0, 3).reshape(j_local, occ_total // 2, 2 * c_local, vir_total)
    narrow, cycle = lax.optimization_barrier((narrow, cycle))

    i_mine = lax.dynamic_index_in_dim(i_labels, pair // halves, keepdims=False)
    a_mine = lax.dynamic_slice_in_dim(vir, fold * a_local + (pair % halves) * a_part, a_part)
    x = (i_mine ^ occ[:, None] ^ a_mine[None, :]).reshape(n_pair, k_local * a_part, 1)
    a_rows = -(-a_part // 8) * 8
    room = -(-k_local * a_part // 16) * 16
    row = jnp.arange(kappas * a_rows, dtype=jnp.int32)[:, None]
    k_kappa = jnp.repeat(kappa, a_part).reshape(n_pair, -1)
    k_kappa = jnp.pad(k_kappa, ((0, 0), (0, room - k_kappa.shape[1])), constant_values=-1).reshape(1, -1)
    column = jnp.arange(n_pair * room, dtype=jnp.int32)[None, :] % room % a_part
    to_row = ((row // a_rows == k_kappa) & (row % a_rows == column)).astype(BF16)
    short = narrow_k(narrow, to_place, x, vir[None, :], to_row, n_fold, a_part, c_local)
    short = lax.all_to_all(short, "fold", split_axis=0, concat_axis=0, tiled=True)

    code = (vir * vmax + vir_place)[None, :, None]
    spots = jnp.arange(irreps * vmax, dtype=jnp.int32).reshape(irreps, 1, vmax)
    picks = (code == spots).astype(BF16)
    inside = starts % a_local
    bounds = [starts // a_local * a_part + jnp.clip(inside - h * a_part, 0, a_part) for h in range(halves)]
    scalars = jnp.concatenate([i_labels, k_from // 2, j_labels] + bounds + [own_vir, pair[None]]).astype(jnp.int32)
    low = n_i + irreps + j_local
    me = low + halves * (irreps + 1) + c_local
    c_label = jnp.broadcast_to(jnp.tile(own_vir.astype(F32), 2)[:, None], (2 * c_local, vir_total)).astype(BF16)
    blocks = class_blocks(
        scalars, cycle, c_label, picks, n_i=n_i, irreps=irreps, owns=low + halves * (irreps + 1), k_pairs=kappas // 2
    )
    short, blocks = lax.optimization_barrier((short, blocks))

    short = short.reshape(n_fold * a_part, kappas * c_local)
    lhs = gather_pieces(short, n_pair)

    most = min(vmax, -(-vmax // a_local) * a_part)
    window = min(-(-(most + 15) // 16) * 16, n_fold * a_part)
    coded = grouped_product(
        scalars, lhs, blocks, n_fold, n_pair, bounds=low, irreps=irreps, halves=halves, window=window, me=me
    )
    coded = lax.all_to_all(coded, "fold", split_axis=0, concat_axis=0, tiled=True).astype(F32)
    shares = coded[:, :-8] * (jnp.exp2(coded[:, -8:-7] * 0.25) / TOP)
    total = jnp.sum(shares, axis=0).astype(BF16).reshape(n_i, a_part, halves, j_local, vmax)
    total = total.transpose(0, 2, 1, 3, 4).reshape(n_i, a_local, j_local, vmax)
    spread_b = pick(total, "iajt,tb->iajb", to_place)
    x = i_labels[:, None, None] ^ own_vir[None, :, None] ^ j_labels[None, None, :]
    return jnp.where(x[..., None] == vir, spread_b, jnp.zeros_like(spread_b))


def solution(mesh):
    placed = (P(None, "pair", "fold", None), P("fold", None, "pair", None), P(), P(), P(), P())
    return jax.shard_map(
        body, mesh=mesh, in_specs=placed, out_specs=P(None, "fold", "pair", None), check_vma=False
    )
```

```python
import functools
import math

import jax
import jax.numpy as jnp
from jax import lax
from jax.experimental import pallas as pl
from jax.experimental.pallas import tpu as pltpu
from jax.sharding import PartitionSpec as P

BF16, F32 = jnp.bfloat16, jnp.float32
TOP = 32767.0


def irrep_labels(sizes, count):
    order = jnp.arange(sizes.shape[1], dtype=jnp.int32)
    positions = jnp.arange(count, dtype=jnp.int32)
    ends = jnp.sum(jnp.where(order[None, None, :] <= order[None, :, None], sizes[:, None, :], 0), axis=2)
    after = positions[None, :, None] >= ends[:, None, :]
    labels = jnp.sum(after.astype(jnp.int32), axis=2)
    places = positions - jnp.sum(jnp.where(after, sizes[:, None, :], 0), axis=2)
    return labels, places, jnp.concatenate([jnp.zeros((sizes.shape[0], 1), jnp.int32), ends], axis=1)


def label_lookup(orbitals, labels, count):
    matches = orbitals[:, None] == jnp.arange(count, dtype=jnp.int32)[None, :]
    return jnp.sum(jnp.where(matches, labels[None, :], 0), axis=1)


def one_hot_rows(places, width):
    return (jnp.arange(width, dtype=jnp.int32)[:, None] == places[None, :]).astype(BF16)


def pick(x, spec, y):
    return jnp.einsum(spec, x, y, preferred_element_type=F32).astype(BF16)


def tile_spans(c_local):
    spans = []
    for first in range(0, 2 * c_local, 16):
        runs = []
        for row in range(first, first + 16):
            c = row % c_local
            if runs and c == runs[-1][1] + 1:
                runs[-1][1] = c
            else:
                runs.append([c, c])
        spans.append(runs)
    return spans


def block_kernel(scalars, cycle, c_label, picks, out, chosen, *, n_i, irreps, owns, first_class):
    step = pl.program_id(0) + first_class
    n_j, _, pair_rows, vir_total = cycle.shape
    k_pairs, width = chosen.shape[1], picks.shape[2]
    for tile, runs in enumerate(tile_spans(pair_rows // 2)):
        rows = slice(16 * tile, 16 * tile + 16)

        def place(h, _):
            first = scalars[n_i + (step ^ h)]
            own = c_label[rows, :] == h.astype(F32).astype(BF16)
            own = jnp.broadcast_to(own[None], (k_pairs,) + own.shape)
            for j in range(n_j):
                chosen[j, :, rows, :] = jnp.where(
                    own, cycle[j, pl.ds(first, k_pairs), rows, :], chosen[j, :, rows, :]
                )
            return 0

        for low, high in runs:
            lax.fori_loop(scalars[owns + low], scalars[owns + high] + 1, place, 0)
    for j in range(n_j):
        narrow = jnp.dot(
            chosen[j].reshape(k_pairs * pair_rows, vir_total),
            picks[step ^ scalars[n_i + irreps + j]],
            preferred_element_type=F32,
        )
        out[0, :, j * width:(j + 1) * width] = narrow.astype(BF16)


def class_blocks(scalars, cycle, c_label, picks, first_class, *, n_i, irreps, owns, k_pairs):
    n_j, _, pair_rows, vir_total = cycle.shape
    width = picks.shape[2]
    depth = k_pairs * pair_rows
    return pl.pallas_call(
        functools.partial(block_kernel, n_i=n_i, irreps=irreps, owns=owns, first_class=first_class),
        out_shape=jax.ShapeDtypeStruct((irreps // 2, depth, n_j * width), BF16),
        grid_spec=pltpu.PrefetchScalarGridSpec(
            num_scalar_prefetch=1,
            grid=(irreps // 2,),
            in_specs=[whole(cycle.shape), whole(c_label.shape), whole(picks.shape)],
            out_specs=pl.BlockSpec((1, depth, n_j * width), lambda r, s: (r, 0, 0)),
            scratch_shapes=[pltpu.VMEM((n_j, k_pairs, pair_rows, vir_total), BF16)],
        ),
        compiler_params=pltpu.CompilerParams(vmem_limit_bytes=48 * 2**20),
        cost_estimate=pl.CostEstimate(
            flops=irreps * depth * n_j * vir_total * width, bytes_accessed=11 * 2**20, transcendentals=0
        ),
    )(scalars, cycle, c_label, picks)


def gather_pieces(v, beside, n_pair):
    def send(value, step):
        return lax.ppermute(value, "pair", [(p, (p + step) % n_pair) for p in range(n_pair)])

    half = v.shape[0] // 2
    up, down, beside = lax.optimization_barrier((send(v, 2), send(v, -2), beside))
    far_up, far_down = send(up[:half], 2), send(down[half:], -2)
    pieces = [v, up, down, far_up, far_down]
    return pieces + [lax.ppermute(p, "pair", [(q, q ^ 1) for q in range(n_pair)]) for p in pieces], beside


def grouped_kernel(scalars, *refs, bounds, irreps, halves, window, me):
    pieces, (early, late, out, lhs, rows, total, packed, block, sems) = refs[:10], refs[10:]
    step = pl.program_id(0)

    @pl.when(step == 0)
    def _():
        y, core = scalars[me] // 2, scalars[me] % 2
        half = lhs.shape[1] // 2
        copies = []
        for n, piece in enumerate(pieces):
            away = (0, -1, 1, 2, 2)[n % 5]
            first = half if n % 5 == 4 else 0
            g = lax.rem(y + away + 4, 4) * 2 + (core if n < 5 else 1 - core)
            copies.append(pltpu.make_async_copy(piece, lhs.at[g, pl.ds(first, piece.shape[0]), :], sems.at[n]))
            copies[-1].start()
        for copy in copies:
            copy.wait()

    groups, n_rows, _ = lhs.shape
    n_i, width = groups // halves, block.shape[1]

    @pl.when(step < irreps // 2)
    def _():
        block[...] = early[0]

    @pl.when(step >= irreps // 2)
    def _():
        block[...] = late[0]

    spans = []
    for g in range(groups):
        at = bounds + (g % halves) * (irreps + 1) + (step ^ scalars[g // halves])
        low, high = scalars[at], scalars[at + 1]
        base = pl.multiple_of(jnp.minimum(low // 16 * 16, n_rows - window), 16)
        rows[g * window:(g + 1) * window, :] = lhs[g, pl.ds(base, window), :]
        spans.append((low, high, base))
    product = jnp.dot(rows[...], block[...], preferred_element_type=F32)
    for g, (low, high, base) in enumerate(spans):
        piece = product[g * window:(g + 1) * window]
        row = base + lax.broadcasted_iota(jnp.int32, piece.shape, 0)
        spot = (g, pl.ds(base, window), slice(None))
        total[spot] = jnp.where((row >= low) & (row < high), piece, total[spot])

    @pl.when(step == irreps - 1)
    def _():
        n_fold = out.shape[0]
        part = n_rows // n_fold
        for f in range(n_fold):
            for g in range(groups):
                at, lane = g // halves * part, g % halves * width
                packed[at:at + part, lane:lane + width] = total[g, f * part:(f + 1) * part, :]
            values = packed[...]
            most = jnp.maximum(jnp.max(jnp.abs(values), axis=0, keepdims=True), 1e-30)
            scale = jnp.ceil(jnp.log2(most) * 4.0)
            code = jnp.clip(jnp.round(values * (TOP * jnp.exp2(scale * -0.25))), -TOP, TOP)
            code = jnp.concatenate([code, jnp.broadcast_to(scale, (8, scale.shape[1]))])
            out[f] = code.astype(jnp.int32).astype(jnp.int16)


def narrow_c_kernel(scalars, x, a_label, label, to_place, out, masked, line, *, n_i, a_local):
    i_label = scalars[pl.program_id(0)]
    between = a_label[...] ^ label[...]
    for k in range(masked.shape[0] // a_local):
        rows = slice(k * a_local, (k + 1) * a_local)
        own = between == (i_label ^ scalars[n_i + k])
        masked[rows, :] = jnp.where(own, x[0, k].astype(F32), 0.0)
    narrow = lax.dot_general(
        to_place[...], masked[...].astype(BF16), (((1,), (1,)), ((), ())), preferred_element_type=F32
    )
    halves, rows = out.shape[0], out.shape[2]
    part = a_local // halves
    for h in range(halves):
        for k in range(rows // part):
            line[:, k * part:(k + 1) * part] = narrow[:, k * a_local + h * part:k * a_local + (h + 1) * part]
        out[h] = line[...].astype(BF16)


def narrow_c(scalars, x, a_label, label, to_place, halves):
    n_i, k_local, a_local, vir_total = x.shape
    width = to_place.shape[0]
    rows = k_local * a_local
    return pl.pallas_call(
        functools.partial(narrow_c_kernel, n_i=n_i, a_local=a_local),
        out_shape=jax.ShapeDtypeStruct((n_i * halves, width, rows // halves), BF16),
        grid_spec=pltpu.PrefetchScalarGridSpec(
            num_scalar_prefetch=1,
            grid=(n_i,),
            in_specs=[
                pl.BlockSpec((1, k_local, a_local, vir_total), lambda i, s: (i, 0, 0, 0)),
                whole(a_label.shape),
                whole(label.shape),
                whole(to_place.shape),
            ],
            out_specs=pl.BlockSpec((halves, width, rows // halves), lambda i, s: (i, 0, 0)),
            scratch_shapes=[pltpu.VMEM((rows, vir_total), F32), pltpu.VMEM((width, rows // halves), F32)],
        ),
        compiler_params=pltpu.CompilerParams(vmem_limit_bytes=60 * 2**20),
        cost_estimate=pl.CostEstimate(
            flops=2 * x.size * width, bytes_accessed=3 * 2**20, transcendentals=0
        ),
    )(scalars, x, a_label, label, to_place)


def narrow_k_kernel(x, to_place, row_label, label, to_row, out, wide, short, line):
    n_fold, a_part, depth = out.shape
    a_rows = line.shape[0]
    c_local = wide.shape[1] // n_fold
    sources, _, rows = x.shape
    room = wide.shape[0] // sources
    for p in range(sources):
        spread = lax.dot_general(x[p], to_place[...], (((0,), (0,)), ((), ())), preferred_element_type=F32)
        spread = jnp.where(row_label[p] == label[...], spread, 0.0)
        if room > rows:
            spread = jnp.concatenate([spread, jnp.zeros((room - rows, spread.shape[1]), F32)])
        wide[p * room:(p + 1) * room, :] = spread.astype(BF16)
    short[...] = jnp.dot(to_row[...], wide[...], preferred_element_type=F32)
    for f in range(n_fold):
        for q in range(depth // c_local):
            line[:, q * c_local:(q + 1) * c_local] = (
                short[q * a_rows:(q + 1) * a_rows, f * c_local:(f + 1) * c_local]
            )
        out[f] = line[:a_part, :].astype(BF16)


def narrow_k(x, to_place, row_label, label, to_row, n_fold, a_part, c_local):
    vir_total = label.shape[1]
    a_rows = -(-a_part // 8) * 8
    depth = to_row.shape[0] // a_rows * c_local
    return pl.pallas_call(
        narrow_k_kernel,
        out_shape=jax.ShapeDtypeStruct((n_fold, a_part, depth), BF16),
        scratch_shapes=[
            pltpu.VMEM((to_row.shape[1], vir_total), BF16),
            pltpu.VMEM((to_row.shape[0], vir_total), F32),
            pltpu.VMEM((a_rows, depth), F32),
        ],
        compiler_params=pltpu.CompilerParams(vmem_limit_bytes=32 * 2**20),
        cost_estimate=pl.CostEstimate(
            flops=2 * to_row.size * vir_total, bytes_accessed=3 * 2**20, transcendentals=0
        ),
    )(x, to_place, row_label, label, to_row)


def whole(shape):
    return pl.BlockSpec(shape, lambda r, s: (0,) * len(shape))


def grouped_product(scalars, pieces, early, late, n_fold, groups, *, bounds, irreps, halves, window, me):
    n_rows, depth = pieces[0].shape
    width, half = early.shape[2], early.shape[0]
    n_i = groups // halves
    share = (n_i * n_rows // n_fold, halves * width)
    shape = (n_fold, share[0] + 8, share[1])
    return pl.pallas_call(
        functools.partial(
            grouped_kernel, bounds=bounds, irreps=irreps, halves=halves, window=window, me=me
        ),
        out_shape=jax.ShapeDtypeStruct(shape, jnp.int16),
        grid_spec=pltpu.PrefetchScalarGridSpec(
            num_scalar_prefetch=1,
            grid=(irreps,),
            in_specs=[pl.BlockSpec(memory_space=pl.ANY)] * len(pieces)
            + [
                pl.BlockSpec((1, depth, width), lambda r, s: (jnp.minimum(r, half - 1), 0, 0)),
                pl.BlockSpec((1, depth, width), lambda r, s: (jnp.maximum(r - half, 0), 0, 0)),
            ],
            out_specs=whole(shape),
            scratch_shapes=[
                pltpu.VMEM((groups, n_rows, depth), BF16),
                pltpu.VMEM((groups * window, depth), BF16),
                pltpu.VMEM((groups, n_rows, width), F32),
                pltpu.VMEM(share, F32),
                pltpu.VMEM((depth, width), BF16),
                pltpu.SemaphoreType.DMA((len(pieces),)),
            ],
        ),
        compiler_params=pltpu.CompilerParams(vmem_limit_bytes=48 * 2**20),
        cost_estimate=pl.CostEstimate(
            flops=2 * irreps * groups * window * depth * width, bytes_accessed=13 * 2**20, transcendentals=0
        ),
    )(scalars, *pieces, early, late)


def body(amplitudes, cycle_block, occ_sizes, vir_sizes, window_i, window_occ):
    irreps = occ_sizes.shape[0]
    n_fold, n_pair = lax.axis_size("fold"), lax.axis_size("pair")
    fold, pair = lax.axis_index("fold"), lax.axis_index("pair")
    c_local, occ_total, j_local, vir_total = cycle_block.shape
    n_i, k_local, a_local, _ = amplitudes.shape
    vmax, omax = vir_total // 4, occ_total // 4
    halves = n_pair // n_i
    a_part = a_local // halves

    labels, places, all_starts = irrep_labels(jnp.stack([occ_sizes, vir_sizes]), vir_total)
    occ, vir, vir_place = labels[0, :occ_total], labels[1], places[1]
    occ_starts, starts = all_starts[0], all_starts[1]
    to_place = one_hot_rows(vir_place, vmax)
    kappas = omax + 2 - omax % 2
    k_from = jnp.minimum(occ_starts[:irreps] // 2 * 2, occ_total - kappas)
    own_from = jnp.where(occ[:, None] == jnp.arange(irreps)[None, :], k_from[None, :], 0)
    kappa = jnp.arange(occ_total, dtype=jnp.int32) - jnp.sum(own_from, axis=1)
    to_kappa = one_hot_rows(kappa, kappas)
    own_vir = lax.dynamic_slice_in_dim(vir, fold * c_local, c_local)
    k_own = lax.dynamic_slice_in_dim(occ, pair * k_local, k_local)
    i_labels = label_lookup(window_i, occ, occ_total)
    j_labels = label_lookup(lax.dynamic_slice_in_dim(window_occ, pair * j_local, j_local), occ, occ_total)

    narrow = narrow_c(
        jnp.concatenate([i_labels, k_own]), amplitudes, own_vir[:, None], vir[None, :], to_place, halves
    )
    narrow = lax.all_to_all(narrow, "pair", split_axis=0, concat_axis=0, tiled=True)
    cycle = cycle_block.transpose(2, 1, 0, 3).reshape(j_local, occ_total // 2, 2 * c_local, vir_total)
    narrow, cycle = lax.optimization_barrier((narrow, cycle))

    i_mine = lax.dynamic_index_in_dim(i_labels, pair // halves, keepdims=False)
    a_mine = lax.dynamic_slice_in_dim(vir, fold * a_local + (pair % halves) * a_part, a_part)
    x = (i_mine ^ occ[:, None] ^ a_mine[None, :]).reshape(n_pair, k_local * a_part, 1)
    a_rows = -(-a_part // 8) * 8
    room = -(-k_local * a_part // 16) * 16
    row = jnp.arange(kappas * a_rows, dtype=jnp.int32)[:, None]
    k_kappa = jnp.repeat(kappa, a_part).reshape(n_pair, -1)
    k_kappa = jnp.pad(k_kappa, ((0, 0), (0, room - k_kappa.shape[1])), constant_values=-1).reshape(1, -1)
    column = jnp.arange(n_pair * room, dtype=jnp.int32)[None, :] % room % a_part
    to_row = ((row // a_rows == k_kappa) & (row % a_rows == column)).astype(BF16)
    short = narrow_k(narrow, to_place, x, vir[None, :], to_row, n_fold, a_part, c_local)
    short = lax.all_to_all(short, "fold", split_axis=0, concat_axis=0, tiled=True)

    code = (vir * vmax + vir_place)[None, :, None]
    spots = jnp.arange(irreps * vmax, dtype=jnp.int32).reshape(irreps, 1, vmax)
    picks = (code == spots).astype(BF16)
    inside = starts % a_local
    bounds = [starts // a_local * a_part + jnp.clip(inside - h * a_part, 0, a_part) for h in range(halves)]
    scalars = jnp.concatenate([i_labels, k_from // 2, j_labels] + bounds + [own_vir, pair[None]]).astype(jnp.int32)
    low = n_i + irreps + j_local
    me = low + halves * (irreps + 1) + c_local
    c_label = jnp.broadcast_to(jnp.tile(own_vir.astype(F32), 2)[:, None], (2 * c_local, vir_total)).astype(BF16)
    make_blocks = functools.partial(
        class_blocks, n_i=n_i, irreps=irreps, owns=low + halves * (irreps + 1), k_pairs=kappas // 2
    )
    early = make_blocks(scalars, cycle, c_label, picks, 0)
    short, early = lax.optimization_barrier((short, early))
    late = make_blocks(scalars, cycle, c_label, picks, irreps // 2)

    short = short.reshape(n_fold * a_part, kappas * c_local)
    lhs, late = gather_pieces(short, late, n_pair)

    most = min(vmax, -(-vmax // a_local) * a_part)
    window = min(-(-(most + 15) // 16) * 16, n_fold * a_part)
    coded = grouped_product(
        scalars, lhs, early, late, n_fold, n_pair, bounds=low, irreps=irreps, halves=halves, window=window, me=me
    )
    coded = lax.all_to_all(coded, "fold", split_axis=0, concat_axis=0, tiled=True).astype(F32)
    shares = coded[:, :-8] * (jnp.exp2(coded[:, -8:-7] * 0.25) / TOP)
    total = jnp.sum(shares, axis=0).astype(BF16).reshape(n_i, a_part, halves, j_local, vmax)
    total = total.transpose(0, 2, 1, 3, 4).reshape(n_i, a_local, j_local, vmax)
    spread_b = pick(total, "iajt,tb->iajb", to_place)
    x = i_labels[:, None, None] ^ own_vir[None, :, None] ^ j_labels[None, None, :]
    return jnp.where(x[..., None] == vir, spread_b, jnp.zeros_like(spread_b))


def solution(mesh):
    placed = (P(None, "pair", "fold", None), P("fold", None, "pair", None), P(), P(), P(), P())
    return jax.shard_map(
        body, mesh=mesh, in_specs=placed, out_specs=P(None, "fold", "pair", None), check_vma=False
    )
```

```python
import functools
import math

import jax
import jax.numpy as jnp
from jax import lax
from jax.experimental import pallas as pl
from jax.experimental.pallas import tpu as pltpu
from jax.sharding import PartitionSpec as P

BF16, F32 = jnp.bfloat16, jnp.float32
TOP = 32767.0


def irrep_labels(sizes, count):
    order = jnp.arange(sizes.shape[1], dtype=jnp.int32)
    positions = jnp.arange(count, dtype=jnp.int32)
    ends = jnp.sum(jnp.where(order[None, None, :] <= order[None, :, None], sizes[:, None, :], 0), axis=2)
    after = positions[None, :, None] >= ends[:, None, :]
    labels = jnp.sum(after.astype(jnp.int32), axis=2)
    places = positions - jnp.sum(jnp.where(after, sizes[:, None, :], 0), axis=2)
    return labels, places, jnp.concatenate([jnp.zeros((sizes.shape[0], 1), jnp.int32), ends], axis=1)


def label_lookup(orbitals, labels, count):
    matches = orbitals[:, None] == jnp.arange(count, dtype=jnp.int32)[None, :]
    return jnp.sum(jnp.where(matches, labels[None, :], 0), axis=1)


def one_hot_rows(places, width):
    return (jnp.arange(width, dtype=jnp.int32)[:, None] == places[None, :]).astype(BF16)


def pick(x, spec, y):
    return jnp.einsum(spec, x, y, preferred_element_type=F32).astype(BF16)


def tile_spans(c_local):
    spans = []
    for first in range(0, 2 * c_local, 16):
        runs = []
        for row in range(first, first + 16):
            c = row % c_local
            if runs and c == runs[-1][1] + 1:
                runs[-1][1] = c
            else:
                runs.append([c, c])
        spans.append(runs)
    return spans


def block_kernel(scalars, cycle, c_label, picks, out, chosen, *, n_i, irreps, owns, first_class):
    step = pl.program_id(0) + first_class
    n_j, _, pair_rows, vir_total = cycle.shape
    k_pairs, width = chosen.shape[1], picks.shape[2]
    for tile, runs in enumerate(tile_spans(pair_rows // 2)):
        rows = slice(16 * tile, 16 * tile + 16)

        def place(h, _):
            first = scalars[n_i + (step ^ h)]
            own = c_label[rows, :] == h.astype(F32).astype(BF16)
            own = jnp.broadcast_to(own[None], (k_pairs,) + own.shape)
            for j in range(n_j):
                chosen[j, :, rows, :] = jnp.where(
                    own, cycle[j, pl.ds(first, k_pairs), rows, :], chosen[j, :, rows, :]
                )
            return 0

        for low, high in runs:
            lax.fori_loop(scalars[owns + low], scalars[owns + high] + 1, place, 0)
    for j in range(n_j):
        narrow = jnp.dot(
            chosen[j].reshape(k_pairs * pair_rows, vir_total),
            picks[step ^ scalars[n_i + irreps + j]],
            preferred_element_type=F32,
        )
        out[0, :, j * width:(j + 1) * width] = narrow.astype(BF16)


def class_blocks(scalars, cycle, c_label, picks, first_class, *, n_i, irreps, owns, k_pairs):
    n_j, _, pair_rows, vir_total = cycle.shape
    width = picks.shape[2]
    depth = k_pairs * pair_rows
    return pl.pallas_call(
        functools.partial(block_kernel, n_i=n_i, irreps=irreps, owns=owns, first_class=first_class),
        out_shape=jax.ShapeDtypeStruct((irreps // 2, depth, n_j * width), BF16),
        grid_spec=pltpu.PrefetchScalarGridSpec(
            num_scalar_prefetch=1,
            grid=(irreps // 2,),
            in_specs=[whole(cycle.shape), whole(c_label.shape), whole(picks.shape)],
            out_specs=pl.BlockSpec((1, depth, n_j * width), lambda r, s: (r, 0, 0)),
            scratch_shapes=[pltpu.VMEM((n_j, k_pairs, pair_rows, vir_total), BF16)],
        ),
        compiler_params=pltpu.CompilerParams(vmem_limit_bytes=60 * 2**20),
        cost_estimate=pl.CostEstimate(
            flops=irreps * depth * n_j * vir_total * width, bytes_accessed=11 * 2**20, transcendentals=0
        ),
    )(scalars, cycle, c_label, picks)


def gather_pieces(v, beside, n_pair):
    def send(value, step):
        return lax.ppermute(value, "pair", [(p, (p + step) % n_pair) for p in range(n_pair)])

    half = v.shape[0] // 2
    upper, lower = v[:half], v[half:]
    up_first, down_first = send(upper, 2), send(lower, -2)
    up_then, down_then = send(lower, 2), send(upper, -2)
    up_first, down_first, beside = lax.optimization_barrier((up_first, down_first, beside))
    far_up, far_down = send(up_first, 2), send(down_first, -2)
    pieces = [v, up_first, up_then, down_then, down_first, far_up, far_down]
    return pieces + [lax.ppermute(p, "pair", [(q, q ^ 1) for q in range(n_pair)]) for p in pieces], beside


def grouped_kernel(scalars, *refs, bounds, irreps, halves, window, me):
    pieces, (early, late, out, lhs, rows, total, packed, block, sems) = refs[:14], refs[14:]
    step = pl.program_id(0)

    @pl.when(step == 0)
    def _():
        y, core = scalars[me] // 2, scalars[me] % 2
        half = lhs.shape[1] // 2
        copies = []
        for n, piece in enumerate(pieces):
            away = (0, -1, -1, 1, 1, 2, 2)[n % 7]
            first = half if n % 7 in (2, 4, 6) else 0
            g = lax.rem(y + away + 4, 4) * 2 + (core if n < 7 else 1 - core)
            copies.append(pltpu.make_async_copy(piece, lhs.at[g, pl.ds(first, piece.shape[0]), :], sems.at[n]))
            copies[-1].start()
        for copy in copies:
            copy.wait()

    groups, n_rows, _ = lhs.shape
    n_i, width = groups // halves, block.shape[1]

    @pl.when(step < irreps // 2)
    def _():
        block[...] = early[0]

    @pl.when(step >= irreps // 2)
    def _():
        block[...] = late[0]

    spans = []
    for g in range(groups):
        at = bounds + (g % halves) * (irreps + 1) + (step ^ scalars[g // halves])
        low, high = scalars[at], scalars[at + 1]
        base = pl.multiple_of(jnp.minimum(low // 16 * 16, n_rows - window), 16)
        rows[g * window:(g + 1) * window, :] = lhs[g, pl.ds(base, window), :]
        spans.append((low, high, base))
    product = jnp.dot(rows[...], block[...], preferred_element_type=F32)
    for g, (low, high, base) in enumerate(spans):
        piece = product[g * window:(g + 1) * window]
        row = base + lax.broadcasted_iota(jnp.int32, piece.shape, 0)
        spot = (g, pl.ds(base, window), slice(None))
        total[spot] = jnp.where((row >= low) & (row < high), piece, total[spot])

    @pl.when(step == irreps - 1)
    def _():
        n_fold = out.shape[0]
        part = n_rows // n_fold
        for f in range(n_fold):
            for g in range(groups):
                at, lane = g // halves * part, g % halves * width
                packed[at:at + part, lane:lane + width] = total[g, f * part:(f + 1) * part, :]
            values = packed[...]
            most = jnp.maximum(jnp.max(jnp.abs(values), axis=0, keepdims=True), 1e-30)
            scale = jnp.ceil(jnp.log2(most) * 4.0)
            code = jnp.clip(jnp.round(values * (TOP * jnp.exp2(scale * -0.25))), -TOP, TOP)
            code = jnp.concatenate([code, jnp.broadcast_to(scale, (8, scale.shape[1]))])
            out[f] = code.astype(jnp.int32).astype(jnp.int16)


def narrow_c_kernel(scalars, x, a_label, label, to_place, out, masked, line, *, n_i, a_local):
    i_label = scalars[pl.program_id(0)]
    between = a_label[...] ^ label[...]
    for k in range(masked.shape[0] // a_local):
        rows = slice(k * a_local, (k + 1) * a_local)
        own = between == (i_label ^ scalars[n_i + k])
        masked[rows, :] = jnp.where(own, x[0, k].astype(F32), 0.0)
    narrow = lax.dot_general(
        to_place[...], masked[...].astype(BF16), (((1,), (1,)), ((), ())), preferred_element_type=F32
    )
    halves, rows = out.shape[0], out.shape[2]
    part = a_local // halves
    for h in range(halves):
        for k in range(rows // part):
            line[:, k * part:(k + 1) * part] = narrow[:, k * a_local + h * part:k * a_local + (h + 1) * part]
        out[h] = line[...].astype(BF16)


def narrow_c(scalars, x, a_label, label, to_place, halves):
    n_i, k_local, a_local, vir_total = x.shape
    width = to_place.shape[0]
    rows = k_local * a_local
    return pl.pallas_call(
        functools.partial(narrow_c_kernel, n_i=n_i, a_local=a_local),
        out_shape=jax.ShapeDtypeStruct((n_i * halves, width, rows // halves), BF16),
        grid_spec=pltpu.PrefetchScalarGridSpec(
            num_scalar_prefetch=1,
            grid=(n_i,),
            in_specs=[
                pl.BlockSpec((1, k_local, a_local, vir_total), lambda i, s: (i, 0, 0, 0)),
                whole(a_label.shape),
                whole(label.shape),
                whole(to_place.shape),
            ],
            out_specs=pl.BlockSpec((halves, width, rows // halves), lambda i, s: (i, 0, 0)),
            scratch_shapes=[pltpu.VMEM((rows, vir_total), F32), pltpu.VMEM((width, rows // halves), F32)],
        ),
        compiler_params=pltpu.CompilerParams(vmem_limit_bytes=32 * 2**20),
        cost_estimate=pl.CostEstimate(
            flops=2 * x.size * width, bytes_accessed=3 * 2**20, transcendentals=0
        ),
    )(scalars, x, a_label, label, to_place)


def narrow_k_kernel(x, to_place, row_label, label, to_row, out, wide, short, line):
    n_fold, a_part, depth = out.shape
    a_rows = line.shape[0]
    c_local = wide.shape[1] // n_fold
    sources, _, rows = x.shape
    room = wide.shape[0] // sources
    for p in range(sources):
        spread = lax.dot_general(x[p], to_place[...], (((0,), (0,)), ((), ())), preferred_element_type=F32)
        spread = jnp.where(row_label[p] == label[...], spread, 0.0)
        if room > rows:
            spread = jnp.concatenate([spread, jnp.zeros((room - rows, spread.shape[1]), F32)])
        wide[p * room:(p + 1) * room, :] = spread.astype(BF16)
    short[...] = jnp.dot(to_row[...], wide[...], preferred_element_type=F32)
    for f in range(n_fold):
        for q in range(depth // c_local):
            line[:, q * c_local:(q + 1) * c_local] = (
                short[q * a_rows:(q + 1) * a_rows, f * c_local:(f + 1) * c_local]
            )
        out[f] = line[:a_part, :].astype(BF16)


def narrow_k(x, to_place, row_label, label, to_row, n_fold, a_part, c_local):
    vir_total = label.shape[1]
    a_rows = -(-a_part // 8) * 8
    depth = to_row.shape[0] // a_rows * c_local
    return pl.pallas_call(
        narrow_k_kernel,
        out_shape=jax.ShapeDtypeStruct((n_fold, a_part, depth), BF16),
        scratch_shapes=[
            pltpu.VMEM((to_row.shape[1], vir_total), BF16),
            pltpu.VMEM((to_row.shape[0], vir_total), F32),
            pltpu.VMEM((a_rows, depth), F32),
        ],
        compiler_params=pltpu.CompilerParams(vmem_limit_bytes=32 * 2**20),
        cost_estimate=pl.CostEstimate(
            flops=2 * to_row.size * vir_total, bytes_accessed=3 * 2**20, transcendentals=0
        ),
    )(x, to_place, row_label, label, to_row)


def whole(shape):
    return pl.BlockSpec(shape, lambda r, s: (0,) * len(shape))


def grouped_product(scalars, pieces, early, late, n_fold, groups, *, bounds, irreps, halves, window, me):
    n_rows, depth = pieces[0].shape
    width, half = early.shape[2], early.shape[0]
    n_i = groups // halves
    share = (n_i * n_rows // n_fold, halves * width)
    shape = (n_fold, share[0] + 8, share[1])
    return pl.pallas_call(
        functools.partial(
            grouped_kernel, bounds=bounds, irreps=irreps, halves=halves, window=window, me=me
        ),
        out_shape=jax.ShapeDtypeStruct(shape, jnp.int16),
        grid_spec=pltpu.PrefetchScalarGridSpec(
            num_scalar_prefetch=1,
            grid=(irreps,),
            in_specs=[pl.BlockSpec(memory_space=pl.ANY)] * len(pieces)
            + [
                pl.BlockSpec((1, depth, width), lambda r, s: (jnp.minimum(r, half - 1), 0, 0)),
                pl.BlockSpec((1, depth, width), lambda r, s: (jnp.maximum(r - half, 0), 0, 0)),
            ],
            out_specs=whole(shape),
            scratch_shapes=[
                pltpu.VMEM((groups, n_rows, depth), BF16),
                pltpu.VMEM((groups * window, depth), BF16),
                pltpu.VMEM((groups, n_rows, width), F32),
                pltpu.VMEM(share, F32),
                pltpu.VMEM((depth, width), BF16),
                pltpu.SemaphoreType.DMA((len(pieces),)),
            ],
        ),
        compiler_params=pltpu.CompilerParams(vmem_limit_bytes=48 * 2**20),
        cost_estimate=pl.CostEstimate(
            flops=2 * irreps * groups * window * depth * width, bytes_accessed=13 * 2**20, transcendentals=0
        ),
    )(scalars, *pieces, early, late)


def body(amplitudes, cycle_block, occ_sizes, vir_sizes, window_i, window_occ):
    irreps = occ_sizes.shape[0]
    n_fold, n_pair = lax.axis_size("fold"), lax.axis_size("pair")
    fold, pair = lax.axis_index("fold"), lax.axis_index("pair")
    c_local, occ_total, j_local, vir_total = cycle_block.shape
    n_i, k_local, a_local, _ = amplitudes.shape
    vmax, omax = vir_total // 4, occ_total // 4
    halves = n_pair // n_i
    a_part = a_local // halves

    labels, places, all_starts = irrep_labels(jnp.stack([occ_sizes, vir_sizes]), vir_total)
    occ, vir, vir_place = labels[0, :occ_total], labels[1], places[1]
    occ_starts, starts = all_starts[0], all_starts[1]
    to_place = one_hot_rows(vir_place, vmax)
    kappas = omax + 2 - omax % 2
    k_from = jnp.minimum(occ_starts[:irreps] // 2 * 2, occ_total - kappas)
    own_from = jnp.where(occ[:, None] == jnp.arange(irreps)[None, :], k_from[None, :], 0)
    kappa = jnp.arange(occ_total, dtype=jnp.int32) - jnp.sum(own_from, axis=1)
    to_kappa = one_hot_rows(kappa, kappas)
    own_vir = lax.dynamic_slice_in_dim(vir, fold * c_local, c_local)
    k_own = lax.dynamic_slice_in_dim(occ, pair * k_local, k_local)
    i_labels = label_lookup(window_i, occ, occ_total)
    j_labels = label_lookup(lax.dynamic_slice_in_dim(window_occ, pair * j_local, j_local), occ, occ_total)

    narrow = narrow_c(
        jnp.concatenate([i_labels, k_own]), amplitudes, own_vir[:, None], vir[None, :], to_place, halves
    )
    narrow = lax.all_to_all(narrow, "pair", split_axis=0, concat_axis=0, tiled=True)
    cycle = cycle_block.transpose(2, 1, 0, 3).reshape(j_local, occ_total // 2, 2 * c_local, vir_total)
    narrow, cycle = lax.optimization_barrier((narrow, cycle))

    i_mine = lax.dynamic_index_in_dim(i_labels, pair // halves, keepdims=False)
    a_mine = lax.dynamic_slice_in_dim(vir, fold * a_local + (pair % halves) * a_part, a_part)
    x = (i_mine ^ occ[:, None] ^ a_mine[None, :]).reshape(n_pair, k_local * a_part, 1)
    a_rows = -(-a_part // 8) * 8
    room = -(-k_local * a_part // 16) * 16
    row = jnp.arange(kappas * a_rows, dtype=jnp.int32)[:, None]
    k_kappa = jnp.repeat(kappa, a_part).reshape(n_pair, -1)
    k_kappa = jnp.pad(k_kappa, ((0, 0), (0, room - k_kappa.shape[1])), constant_values=-1).reshape(1, -1)
    column = jnp.arange(n_pair * room, dtype=jnp.int32)[None, :] % room % a_part
    to_row = ((row // a_rows == k_kappa) & (row % a_rows == column)).astype(BF16)
    short = narrow_k(narrow, to_place, x, vir[None, :], to_row, n_fold, a_part, c_local)
    short = lax.all_to_all(short, "fold", split_axis=0, concat_axis=0, tiled=True)

    code = (vir * vmax + vir_place)[None, :, None]
    spots = jnp.arange(irreps * vmax, dtype=jnp.int32).reshape(irreps, 1, vmax)
    picks = (code == spots).astype(BF16)
    inside = starts % a_local
    bounds = [starts // a_local * a_part + jnp.clip(inside - h * a_part, 0, a_part) for h in range(halves)]
    scalars = jnp.concatenate([i_labels, k_from // 2, j_labels] + bounds + [own_vir, pair[None]]).astype(jnp.int32)
    low = n_i + irreps + j_local
    me = low + halves * (irreps + 1) + c_local
    c_label = jnp.broadcast_to(jnp.tile(own_vir.astype(F32), 2)[:, None], (2 * c_local, vir_total)).astype(BF16)
    make_blocks = functools.partial(
        class_blocks, n_i=n_i, irreps=irreps, owns=low + halves * (irreps + 1), k_pairs=kappas // 2
    )
    early = make_blocks(scalars, cycle, c_label, picks, 0)
    short, early = lax.optimization_barrier((short, early))
    late = make_blocks(scalars, cycle, c_label, picks, irreps // 2)

    short = short.reshape(n_fold * a_part, kappas * c_local)
    lhs, late = gather_pieces(short, late, n_pair)

    most = min(vmax, -(-vmax // a_local) * a_part)
    window = min(-(-(most + 15) // 16) * 16, n_fold * a_part)
    coded = grouped_product(
        scalars, lhs, early, late, n_fold, n_pair, bounds=low, irreps=irreps, halves=halves, window=window, me=me
    )
    coded = lax.all_to_all(coded, "fold", split_axis=0, concat_axis=0, tiled=True).astype(F32)
    shares = coded[:, :-8] * (jnp.exp2(coded[:, -8:-7] * 0.25) / TOP)
    total = jnp.sum(shares, axis=0).astype(BF16).reshape(n_i, a_part, halves, j_local, vmax)
    total = total.transpose(0, 2, 1, 3, 4).reshape(n_i, a_local, j_local, vmax)
    spread_b = pick(total, "iajt,tb->iajb", to_place)
    x = i_labels[:, None, None] ^ own_vir[None, :, None] ^ j_labels[None, None, :]
    return jnp.where(x[..., None] == vir, spread_b, jnp.zeros_like(spread_b))


def solution(mesh):
    placed = (P(None, "pair", "fold", None), P("fold", None, "pair", None), P(), P(), P(), P())
    return jax.shard_map(
        body, mesh=mesh, in_specs=placed, out_specs=P(None, "fold", "pair", None), check_vma=False
    )
```

```python
import functools
import math

import jax
import jax.numpy as jnp
from jax import lax
from jax.experimental import pallas as pl
from jax.experimental.pallas import tpu as pltpu
from jax.sharding import PartitionSpec as P

BF16, F32 = jnp.bfloat16, jnp.float32
TOP = 32767.0


def irrep_labels(sizes, count):
    order = jnp.arange(sizes.shape[1], dtype=jnp.int32)
    positions = jnp.arange(count, dtype=jnp.int32)
    ends = jnp.sum(jnp.where(order[None, None, :] <= order[None, :, None], sizes[:, None, :], 0), axis=2)
    after = positions[None, :, None] >= ends[:, None, :]
    labels = jnp.sum(after.astype(jnp.int32), axis=2)
    places = positions - jnp.sum(jnp.where(after, sizes[:, None, :], 0), axis=2)
    return labels, places, jnp.concatenate([jnp.zeros((sizes.shape[0], 1), jnp.int32), ends], axis=1)


def label_lookup(orbitals, labels, count):
    matches = orbitals[:, None] == jnp.arange(count, dtype=jnp.int32)[None, :]
    return jnp.sum(jnp.where(matches, labels[None, :], 0), axis=1)


def one_hot_rows(places, width):
    return (jnp.arange(width, dtype=jnp.int32)[:, None] == places[None, :]).astype(BF16)


def pick(x, spec, y):
    return jnp.einsum(spec, x, y, preferred_element_type=F32).astype(BF16)


def tile_spans(c_local):
    spans = []
    for first in range(0, 2 * c_local, 16):
        runs = []
        for row in range(first, first + 16):
            c = row % c_local
            if runs and c == runs[-1][1] + 1:
                runs[-1][1] = c
            else:
                runs.append([c, c])
        spans.append(runs)
    return spans


def block_kernel(scalars, cycle, c_label, picks, out, chosen, *, n_i, irreps, owns):
    step = pl.program_id(0)
    n_j, _, pair_rows, vir_total = cycle.shape
    k_pairs, width = chosen.shape[1], picks.shape[2]
    for tile, runs in enumerate(tile_spans(pair_rows // 2)):
        rows = slice(16 * tile, 16 * tile + 16)

        def place(h, _):
            first = scalars[n_i + (step ^ h)]
            own = c_label[rows, :] == h.astype(F32).astype(BF16)
            own = jnp.broadcast_to(own[None], (k_pairs,) + own.shape)
            for j in range(n_j):
                chosen[j, :, rows, :] = jnp.where(
                    own, cycle[j, pl.ds(first, k_pairs), rows, :], chosen[j, :, rows, :]
                )
            return 0

        for low, high in runs:
            lax.fori_loop(scalars[owns + low], scalars[owns + high] + 1, place, 0)
    for j in range(n_j):
        narrow = jnp.dot(
            chosen[j].reshape(k_pairs * pair_rows, vir_total),
            picks[step ^ scalars[n_i + irreps + j]],
            preferred_element_type=F32,
        )
        out[0, :, j * width:(j + 1) * width] = narrow.astype(BF16)


def class_blocks(scalars, cycle, c_label, picks, *, n_i, irreps, owns, k_pairs):
    n_j, _, pair_rows, vir_total = cycle.shape
    width = picks.shape[2]
    depth = k_pairs * pair_rows
    return pl.pallas_call(
        functools.partial(block_kernel, n_i=n_i, irreps=irreps, owns=owns),
        out_shape=jax.ShapeDtypeStruct((irreps, depth, n_j * width), BF16),
        grid_spec=pltpu.PrefetchScalarGridSpec(
            num_scalar_prefetch=1,
            grid=(irreps,),
            in_specs=[whole(cycle.shape), whole(c_label.shape), whole(picks.shape)],
            out_specs=pl.BlockSpec((1, depth, n_j * width), lambda r, s: (r, 0, 0)),
            scratch_shapes=[pltpu.VMEM((n_j, k_pairs, pair_rows, vir_total), BF16)],
        ),
        compiler_params=pltpu.CompilerParams(vmem_limit_bytes=48 * 2**20),
        cost_estimate=pl.CostEstimate(
            flops=2 * irreps * depth * n_j * vir_total * width, bytes_accessed=14 * 2**20, transcendentals=0
        ),
    )(scalars, cycle, c_label, picks)


def gather_pieces(v, beside, n_pair):
    def send(value, step):
        return lax.ppermute(value, "pair", [(p, (p + step) % n_pair) for p in range(n_pair)])

    half = v.shape[0] // 2
    up, down, beside = lax.optimization_barrier((send(v, 2), send(v, -2), beside))
    far_up, far_down = send(up[:half], 2), send(down[half:], -2)
    pieces = [v, up, down, far_up, far_down]
    return pieces + [lax.ppermute(p, "pair", [(q, q ^ 1) for q in range(n_pair)]) for p in pieces], beside


def grouped_kernel(scalars, *refs, bounds, irreps, halves, window, me):
    pieces, (block, out, lhs, rows, total, packed, sems) = refs[:10], refs[10:]
    step = pl.program_id(0)

    @pl.when(step == 0)
    def _():
        y, core = scalars[me] // 2, scalars[me] % 2
        half = lhs.shape[1] // 2
        copies = []
        for n, piece in enumerate(pieces):
            away = (0, -1, 1, 2, 2)[n % 5]
            first = half if n % 5 == 4 else 0
            g = lax.rem(y + away + 4, 4) * 2 + (core if n < 5 else 1 - core)
            copies.append(pltpu.make_async_copy(piece, lhs.at[g, pl.ds(first, piece.shape[0]), :], sems.at[n]))
            copies[-1].start()
        for copy in copies:
            copy.wait()

    groups, n_rows, _ = lhs.shape
    n_i, width = groups // halves, block.shape[2]
    spans = []
    for g in range(groups):
        at = bounds + (g % halves) * (irreps + 1) + (step ^ scalars[g // halves])
        low, high = scalars[at], scalars[at + 1]
        base = pl.multiple_of(jnp.minimum(low // 16 * 16, n_rows - window), 16)
        rows[g * window:(g + 1) * window, :] = lhs[g, pl.ds(base, window), :]
        spans.append((low, high, base))
    product = jnp.dot(rows[...], block[0], preferred_element_type=F32)
    for g, (low, high, base) in enumerate(spans):
        piece = product[g * window:(g + 1) * window]
        row = base + lax.broadcasted_iota(jnp.int32, piece.shape, 0)
        spot = (g, pl.ds(base, window), slice(None))
        total[spot] = jnp.where((row >= low) & (row < high), piece, total[spot])

    @pl.when(step == irreps - 1)
    def _():
        n_fold = out.shape[0]
        part = n_rows // n_fold
        for f in range(n_fold):
            for g in range(groups):
                at, lane = g // halves * part, g % halves * width
                packed[at:at + part, lane:lane + width] = total[g, f * part:(f + 1) * part, :]
            values = packed[...]
            most = jnp.maximum(jnp.max(jnp.abs(values), axis=0, keepdims=True), 1e-30)
            scale = jnp.ceil(jnp.log2(most) * 4.0)
            code = jnp.clip(jnp.round(values * (TOP * jnp.exp2(scale * -0.25))), -TOP, TOP)
            code = jnp.concatenate([code, jnp.broadcast_to(scale, (8, scale.shape[1]))])
            out[f] = code.astype(jnp.int32).astype(jnp.int16)


def narrow_c_kernel(scalars, x, a_label, label, to_place, out, masked, line, *, n_i, a_local):
    i_label = scalars[pl.program_id(0)]
    between = a_label[...] ^ label[...]
    for k in range(masked.shape[0] // a_local):
        rows = slice(k * a_local, (k + 1) * a_local)
        own = between == (i_label ^ scalars[n_i + k])
        masked[rows, :] = jnp.where(own, x[0, k].astype(F32), 0.0)
    narrow = lax.dot_general(
        to_place[...], masked[...].astype(BF16), (((1,), (1,)), ((), ())), preferred_element_type=F32
    )
    halves, rows = out.shape[0], out.shape[2]
    part = a_local // halves
    for h in range(halves):
        for k in range(rows // part):
            line[:, k * part:(k + 1) * part] = narrow[:, k * a_local + h * part:k * a_local + (h + 1) * part]
        out[h] = line[...].astype(BF16)


def narrow_c(scalars, x, a_label, label, to_place, halves):
    n_i, k_local, a_local, vir_total = x.shape
    width = to_place.shape[0]
    rows = k_local * a_local
    return pl.pallas_call(
        functools.partial(narrow_c_kernel, n_i=n_i, a_local=a_local),
        out_shape=jax.ShapeDtypeStruct((n_i * halves, width, rows // halves), BF16),
        grid_spec=pltpu.PrefetchScalarGridSpec(
            num_scalar_prefetch=1,
            grid=(n_i,),
            in_specs=[
                pl.BlockSpec((1, k_local, a_local, vir_total), lambda i, s: (i, 0, 0, 0)),
                whole(a_label.shape),
                whole(label.shape),
                whole(to_place.shape),
            ],
            out_specs=pl.BlockSpec((halves, width, rows // halves), lambda i, s: (i, 0, 0)),
            scratch_shapes=[pltpu.VMEM((rows, vir_total), F32), pltpu.VMEM((width, rows // halves), F32)],
        ),
        compiler_params=pltpu.CompilerParams(vmem_limit_bytes=32 * 2**20),
        cost_estimate=pl.CostEstimate(
            flops=2 * x.size * width, bytes_accessed=3 * 2**20, transcendentals=0
        ),
    )(scalars, x, a_label, label, to_place)


def narrow_k_kernel(x, to_place, row_label, label, to_row, out, wide, short, line):
    n_fold, a_part, depth = out.shape
    a_rows = line.shape[0]
    c_local = wide.shape[1] // n_fold
    sources, _, rows = x.shape
    room = wide.shape[0] // sources
    for p in range(sources):
        spread = lax.dot_general(x[p], to_place[...], (((0,), (0,)), ((), ())), preferred_element_type=F32)
        spread = jnp.where(row_label[p] == label[...], spread, 0.0)
        if room > rows:
            spread = jnp.concatenate([spread, jnp.zeros((room - rows, spread.shape[1]), F32)])
        wide[p * room:(p + 1) * room, :] = spread.astype(BF16)
    short[...] = jnp.dot(to_row[...], wide[...], preferred_element_type=F32)
    for f in range(n_fold):
        for q in range(depth // c_local):
            line[:, q * c_local:(q + 1) * c_local] = (
                short[q * a_rows:(q + 1) * a_rows, f * c_local:(f + 1) * c_local]
            )
        out[f] = line[:a_part, :].astype(BF16)


def narrow_k(x, to_place, row_label, label, to_row, n_fold, a_part, c_local):
    vir_total = label.shape[1]
    a_rows = -(-a_part // 8) * 8
    depth = to_row.shape[0] // a_rows * c_local
    return pl.pallas_call(
        narrow_k_kernel,
        out_shape=jax.ShapeDtypeStruct((n_fold, a_part, depth), BF16),
        scratch_shapes=[
            pltpu.VMEM((to_row.shape[1], vir_total), BF16),
            pltpu.VMEM((to_row.shape[0], vir_total), F32),
            pltpu.VMEM((a_rows, depth), F32),
        ],
        compiler_params=pltpu.CompilerParams(vmem_limit_bytes=32 * 2**20),
        cost_estimate=pl.CostEstimate(
            flops=2 * to_row.size * vir_total, bytes_accessed=3 * 2**20, transcendentals=0
        ),
    )(x, to_place, row_label, label, to_row)


def whole(shape):
    return pl.BlockSpec(shape, lambda r, s: (0,) * len(shape))


def grouped_product(scalars, pieces, block, n_fold, groups, *, bounds, irreps, halves, window, me):
    n_rows, depth = pieces[0].shape
    width = block.shape[2]
    n_i = groups // halves
    share = (n_i * n_rows // n_fold, halves * width)
    shape = (n_fold, share[0] + 8, share[1])
    return pl.pallas_call(
        functools.partial(
            grouped_kernel, bounds=bounds, irreps=irreps, halves=halves, window=window, me=me
        ),
        out_shape=jax.ShapeDtypeStruct(shape, jnp.int16),
        grid_spec=pltpu.PrefetchScalarGridSpec(
            num_scalar_prefetch=1,
            grid=(irreps,),
            in_specs=[pl.BlockSpec(memory_space=pl.ANY)] * len(pieces)
            + [pl.BlockSpec((1, depth, width), lambda r, s: (r, 0, 0))],
            out_specs=whole(shape),
            scratch_shapes=[
                pltpu.VMEM((groups, n_rows, depth), BF16),
                pltpu.VMEM((groups * window, depth), BF16),
                pltpu.VMEM((groups, n_rows, width), F32),
                pltpu.VMEM(share, F32),
                pltpu.SemaphoreType.DMA((len(pieces),)),
            ],
        ),
        compiler_params=pltpu.CompilerParams(vmem_limit_bytes=48 * 2**20),
        cost_estimate=pl.CostEstimate(
            flops=2 * irreps * groups * window * depth * width, bytes_accessed=13 * 2**20, transcendentals=0
        ),
    )(scalars, *pieces, block)


def body(amplitudes, cycle_block, occ_sizes, vir_sizes, window_i, window_occ):
    irreps = occ_sizes.shape[0]
    n_fold, n_pair = lax.axis_size("fold"), lax.axis_size("pair")
    fold, pair = lax.axis_index("fold"), lax.axis_index("pair")
    c_local, occ_total, j_local, vir_total = cycle_block.shape
    n_i, k_local, a_local, _ = amplitudes.shape
    vmax, omax = vir_total // 4, occ_total // 4
    halves = n_pair // n_i
    a_part = a_local // halves

    labels, places, all_starts = irrep_labels(jnp.stack([occ_sizes, vir_sizes]), vir_total)
    occ, vir, vir_place = labels[0, :occ_total], labels[1], places[1]
    occ_starts, starts = all_starts[0], all_starts[1]
    to_place = one_hot_rows(vir_place, vmax)
    kappas = omax + 2 - omax % 2
    k_from = jnp.minimum(occ_starts[:irreps] // 2 * 2, occ_total - kappas)
    own_from = jnp.where(occ[:, None] == jnp.arange(irreps)[None, :], k_from[None, :], 0)
    kappa = jnp.arange(occ_total, dtype=jnp.int32) - jnp.sum(own_from, axis=1)
    to_kappa = one_hot_rows(kappa, kappas)
    own_vir = lax.dynamic_slice_in_dim(vir, fold * c_local, c_local)
    k_own = lax.dynamic_slice_in_dim(occ, pair * k_local, k_local)
    i_labels = label_lookup(window_i, occ, occ_total)
    j_labels = label_lookup(lax.dynamic_slice_in_dim(window_occ, pair * j_local, j_local), occ, occ_total)

    narrow = narrow_c(
        jnp.concatenate([i_labels, k_own]), amplitudes, own_vir[:, None], vir[None, :], to_place, halves
    )
    narrow = lax.all_to_all(narrow, "pair", split_axis=0, concat_axis=0, tiled=True)
    cycle = cycle_block.transpose(2, 1, 0, 3).reshape(j_local, occ_total // 2, 2 * c_local, vir_total)
    narrow, cycle = lax.optimization_barrier((narrow, cycle))

    i_mine = lax.dynamic_index_in_dim(i_labels, pair // halves, keepdims=False)
    a_mine = lax.dynamic_slice_in_dim(vir, fold * a_local + (pair % halves) * a_part, a_part)
    x = (i_mine ^ occ[:, None] ^ a_mine[None, :]).reshape(n_pair, k_local * a_part, 1)
    a_rows = -(-a_part // 8) * 8
    room = -(-k_local * a_part // 16) * 16
    row = jnp.arange(kappas * a_rows, dtype=jnp.int32)[:, None]
    k_kappa = jnp.repeat(kappa, a_part).reshape(n_pair, -1)
    k_kappa = jnp.pad(k_kappa, ((0, 0), (0, room - k_kappa.shape[1])), constant_values=-1).reshape(1, -1)
    column = jnp.arange(n_pair * room, dtype=jnp.int32)[None, :] % room % a_part
    to_row = ((row // a_rows == k_kappa) & (row % a_rows == column)).astype(BF16)
    short = narrow_k(narrow, to_place, x, vir[None, :], to_row, n_fold, a_part, c_local)
    short = lax.all_to_all(short, "fold", split_axis=0, concat_axis=0, tiled=True)

    code = (vir * vmax + vir_place)[None, :, None]
    spots = jnp.arange(irreps * vmax, dtype=jnp.int32).reshape(irreps, 1, vmax)
    picks = (code == spots).astype(BF16)
    inside = starts % a_local
    bounds = [starts // a_local * a_part + jnp.clip(inside - h * a_part, 0, a_part) for h in range(halves)]
    scalars = jnp.concatenate([i_labels, k_from // 2, j_labels] + bounds + [own_vir, pair[None]]).astype(jnp.int32)
    low = n_i + irreps + j_local
    me = low + halves * (irreps + 1) + c_local
    c_label = jnp.broadcast_to(jnp.tile(own_vir.astype(F32), 2)[:, None], (2 * c_local, vir_total)).astype(BF16)
    blocks = class_blocks(
        scalars, cycle, c_label, picks, n_i=n_i, irreps=irreps, owns=low + halves * (irreps + 1), k_pairs=kappas // 2
    )
    short = short.reshape(n_fold * a_part, kappas * c_local)
    lhs, blocks = gather_pieces(short, blocks, n_pair)

    most = min(vmax, -(-vmax // a_local) * a_part)
    window = min(-(-(most + 15) // 16) * 16, n_fold * a_part)
    coded = grouped_product(
        scalars, lhs, blocks, n_fold, n_pair, bounds=low, irreps=irreps, halves=halves, window=window, me=me
    )
    coded = lax.all_to_all(coded, "fold", split_axis=0, concat_axis=0, tiled=True).astype(F32)
    shares = coded[:, :-8] * (jnp.exp2(coded[:, -8:-7] * 0.25) / TOP)
    total = jnp.sum(shares, axis=0).astype(BF16).reshape(n_i, a_part, halves, j_local, vmax)
    total = total.transpose(0, 2, 1, 3, 4).reshape(n_i, a_local, j_local, vmax)
    spread_b = pick(total, "iajt,tb->iajb", to_place)
    x = i_labels[:, None, None] ^ own_vir[None, :, None] ^ j_labels[None, None, :]
    return jnp.where(x[..., None] == vir, spread_b, jnp.zeros_like(spread_b))


def solution(mesh):
    placed = (P(None, "pair", "fold", None), P("fold", None, "pair", None), P(), P(), P(), P())
    return jax.shard_map(
        body, mesh=mesh, in_specs=placed, out_specs=P(None, "fold", "pair", None), check_vma=False
    )
```

```python
import functools
import math

import jax
import jax.numpy as jnp
from jax import lax
from jax.experimental import pallas as pl
from jax.experimental.pallas import tpu as pltpu
from jax.sharding import PartitionSpec as P

BF16, F32 = jnp.bfloat16, jnp.float32
TOP = 32767.0


def irrep_labels(sizes, count):
    order = jnp.arange(sizes.shape[1], dtype=jnp.int32)
    positions = jnp.arange(count, dtype=jnp.int32)
    ends = jnp.sum(jnp.where(order[None, None, :] <= order[None, :, None], sizes[:, None, :], 0), axis=2)
    after = positions[None, :, None] >= ends[:, None, :]
    labels = jnp.sum(after.astype(jnp.int32), axis=2)
    places = positions - jnp.sum(jnp.where(after, sizes[:, None, :], 0), axis=2)
    return labels, places, jnp.concatenate([jnp.zeros((sizes.shape[0], 1), jnp.int32), ends], axis=1)


def label_lookup(orbitals, labels, count):
    matches = orbitals[:, None] == jnp.arange(count, dtype=jnp.int32)[None, :]
    return jnp.sum(jnp.where(matches, labels[None, :], 0), axis=1)


def one_hot_rows(places, width):
    return (jnp.arange(width, dtype=jnp.int32)[:, None] == places[None, :]).astype(BF16)


def pick(x, spec, y):
    return jnp.einsum(spec, x, y, preferred_element_type=F32).astype(BF16)


def tile_spans(c_local):
    spans = []
    for first in range(0, 2 * c_local, 16):
        runs = []
        for row in range(first, first + 16):
            c = row % c_local
            if runs and c == runs[-1][1] + 1:
                runs[-1][1] = c
            else:
                runs.append([c, c])
        spans.append(runs)
    return spans


def block_kernel(scalars, cycle, c_label, picks, out, chosen, *, n_i, irreps, owns):
    step = pl.program_id(0)
    n_j, _, pair_rows, vir_total = cycle.shape
    k_pairs, width = chosen.shape[1], picks.shape[2]
    for tile, runs in enumerate(tile_spans(pair_rows // 2)):
        rows = slice(16 * tile, 16 * tile + 16)

        def place(h, _):
            first = scalars[n_i + (step ^ h)]
            own = c_label[rows, :] == h.astype(F32).astype(BF16)
            own = jnp.broadcast_to(own[None], (k_pairs,) + own.shape)
            for j in range(n_j):
                chosen[j, :, rows, :] = jnp.where(
                    own, cycle[j, pl.ds(first, k_pairs), rows, :], chosen[j, :, rows, :]
                )
            return 0

        for low, high in runs:
            lax.fori_loop(scalars[owns + low], scalars[owns + high] + 1, place, 0)
    for j in range(n_j):
        narrow = jnp.dot(
            chosen[j].reshape(k_pairs * pair_rows, vir_total),
            picks[step ^ scalars[n_i + irreps + j]],
            preferred_element_type=F32,
        )
        out[0, :, j * width:(j + 1) * width] = narrow.astype(BF16)


def class_blocks(scalars, cycle, c_label, picks, *, n_i, irreps, owns, k_pairs):
    n_j, _, pair_rows, vir_total = cycle.shape
    width = picks.shape[2]
    depth = k_pairs * pair_rows
    return pl.pallas_call(
        functools.partial(block_kernel, n_i=n_i, irreps=irreps, owns=owns),
        out_shape=jax.ShapeDtypeStruct((irreps, depth, n_j * width), BF16),
        grid_spec=pltpu.PrefetchScalarGridSpec(
            num_scalar_prefetch=1,
            grid=(irreps,),
            in_specs=[whole(cycle.shape), whole(c_label.shape), whole(picks.shape)],
            out_specs=pl.BlockSpec((1, depth, n_j * width), lambda r, s: (r, 0, 0)),
            scratch_shapes=[pltpu.VMEM((n_j, k_pairs, pair_rows, vir_total), BF16)],
        ),
        compiler_params=pltpu.CompilerParams(vmem_limit_bytes=48 * 2**20),
        cost_estimate=pl.CostEstimate(
            flops=2 * irreps * depth * n_j * vir_total * width, bytes_accessed=14 * 2**20, transcendentals=0
        ),
    )(scalars, cycle, c_label, picks)


def gather_pieces(v, beside, n_pair):
    def send(value, step):
        return lax.ppermute(value, "pair", [(p, (p + step) % n_pair) for p in range(n_pair)])

    half = v.shape[0] // 2
    up, down, beside = lax.optimization_barrier((send(v, 2), send(v, -2), beside))
    far_up, far_down = send(up[:half], 2), send(down[half:], -2)
    pieces = [v, up, down, far_up, far_down]
    return pieces + [lax.ppermute(p, "pair", [(q, q ^ 1) for q in range(n_pair)]) for p in pieces], beside


def grouped_kernel(scalars, *refs, bounds, irreps, halves, window, me):
    pieces, (block, out, lhs, rows, total, packed, sems) = refs[:10], refs[10:]
    step = pl.program_id(0)

    @pl.when(step == 0)
    def _():
        y, core = scalars[me] // 2, scalars[me] % 2
        half = lhs.shape[1] // 2
        copies = []
        for n, piece in enumerate(pieces):
            away = (0, -1, 1, 2, 2)[n % 5]
            first = half if n % 5 == 4 else 0
            g = lax.rem(y + away + 4, 4) * 2 + (core if n < 5 else 1 - core)
            copies.append(pltpu.make_async_copy(piece, lhs.at[g, pl.ds(first, piece.shape[0]), :], sems.at[n]))
            copies[-1].start()
        for copy in copies:
            copy.wait()

    groups, n_rows, _ = lhs.shape
    n_i, width = groups // halves, block.shape[2]
    spans = []
    for g in range(groups):
        at = bounds + (g % halves) * (irreps + 1) + (step ^ scalars[g // halves])
        low, high = scalars[at], scalars[at + 1]
        base = pl.multiple_of(jnp.minimum(low // 16 * 16, n_rows - window), 16)
        rows[g * window:(g + 1) * window, :] = lhs[g, pl.ds(base, window), :]
        spans.append((low, high, base))
    product = jnp.dot(rows[...], block[0], preferred_element_type=F32)
    for g, (low, high, base) in enumerate(spans):
        piece = product[g * window:(g + 1) * window]
        row = base + lax.broadcasted_iota(jnp.int32, piece.shape, 0)
        spot = (g, pl.ds(base, window), slice(None))
        total[spot] = jnp.where((row >= low) & (row < high), piece, total[spot])

    @pl.when(step == irreps - 1)
    def _():
        n_fold = out.shape[0]
        part = n_rows // n_fold
        for f in range(n_fold):
            for g in range(groups):
                at, lane = g // halves * part, g % halves * width
                packed[at:at + part, lane:lane + width] = total[g, f * part:(f + 1) * part, :]
            values = packed[...]
            most = jnp.maximum(jnp.max(jnp.abs(values), axis=0, keepdims=True), 1e-30)
            scale = jnp.ceil(jnp.log2(most) * 4.0)
            code = jnp.clip(jnp.round(values * (TOP * jnp.exp2(scale * -0.25))), -TOP, TOP)
            code = jnp.concatenate([code, jnp.broadcast_to(scale, (8, scale.shape[1]))])
            out[f] = code.astype(jnp.int32).astype(jnp.int16)


def narrow_c_kernel(scalars, x, a_label, label, to_place, out, masked, line, *, n_i, a_local):
    i_label = scalars[pl.program_id(0)]
    between = a_label[...] ^ label[...]
    for k in range(masked.shape[0] // a_local):
        rows = slice(k * a_local, (k + 1) * a_local)
        own = between == (i_label ^ scalars[n_i + k])
        masked[rows, :] = jnp.where(own, x[0, k].astype(F32), 0.0)
    narrow = lax.dot_general(
        to_place[...], masked[...].astype(BF16), (((1,), (1,)), ((), ())), preferred_element_type=F32
    )
    halves, rows = out.shape[0], out.shape[2]
    part = a_local // halves
    for h in range(halves):
        for k in range(rows // part):
            line[:, k * part:(k + 1) * part] = narrow[:, k * a_local + h * part:k * a_local + (h + 1) * part]
        out[h] = line[...].astype(BF16)


def narrow_c(scalars, x, a_label, label, to_place, halves):
    n_i, k_local, a_local, vir_total = x.shape
    width = to_place.shape[0]
    rows = k_local * a_local
    return pl.pallas_call(
        functools.partial(narrow_c_kernel, n_i=n_i, a_local=a_local),
        out_shape=jax.ShapeDtypeStruct((n_i * halves, width, rows // halves), BF16),
        grid_spec=pltpu.PrefetchScalarGridSpec(
            num_scalar_prefetch=1,
            grid=(n_i,),
            in_specs=[
                pl.BlockSpec((1, k_local, a_local, vir_total), lambda i, s: (i, 0, 0, 0)),
                whole(a_label.shape),
                whole(label.shape),
                whole(to_place.shape),
            ],
            out_specs=pl.BlockSpec((halves, width, rows // halves), lambda i, s: (i, 0, 0)),
            scratch_shapes=[pltpu.VMEM((rows, vir_total), F32), pltpu.VMEM((width, rows // halves), F32)],
        ),
        compiler_params=pltpu.CompilerParams(vmem_limit_bytes=32 * 2**20),
        cost_estimate=pl.CostEstimate(
            flops=2 * x.size * width, bytes_accessed=3 * 2**20, transcendentals=0
        ),
    )(scalars, x, a_label, label, to_place)


def narrow_k_kernel(x, to_place, row_label, label, to_row, out, wide, short, line):
    n_fold, a_part, depth = out.shape
    a_rows = line.shape[0]
    c_local = wide.shape[1] // n_fold
    sources, _, rows = x.shape
    room = wide.shape[0] // sources
    for p in range(sources):
        spread = lax.dot_general(x[p], to_place[...], (((0,), (0,)), ((), ())), preferred_element_type=F32)
        spread = jnp.where(row_label[p] == label[...], spread, 0.0)
        if room > rows:
            spread = jnp.concatenate([spread, jnp.zeros((room - rows, spread.shape[1]), F32)])
        wide[p * room:(p + 1) * room, :] = spread.astype(BF16)
    short[...] = jnp.dot(to_row[...], wide[...], preferred_element_type=F32)
    for f in range(n_fold):
        for q in range(depth // c_local):
            line[:, q * c_local:(q + 1) * c_local] = (
                short[q * a_rows:(q + 1) * a_rows, f * c_local:(f + 1) * c_local]
            )
        out[f] = line[:a_part, :].astype(BF16)


def narrow_k(x, to_place, row_label, label, to_row, n_fold, a_part, c_local):
    vir_total = label.shape[1]
    a_rows = -(-a_part // 8) * 8
    depth = to_row.shape[0] // a_rows * c_local
    return pl.pallas_call(
        narrow_k_kernel,
        out_shape=jax.ShapeDtypeStruct((n_fold, a_part, depth), BF16),
        scratch_shapes=[
            pltpu.VMEM((to_row.shape[1], vir_total), BF16),
            pltpu.VMEM((to_row.shape[0], vir_total), F32),
            pltpu.VMEM((a_rows, depth), F32),
        ],
        compiler_params=pltpu.CompilerParams(vmem_limit_bytes=32 * 2**20),
        cost_estimate=pl.CostEstimate(
            flops=2 * to_row.size * vir_total, bytes_accessed=3 * 2**20, transcendentals=0
        ),
    )(x, to_place, row_label, label, to_row)


def whole(shape):
    return pl.BlockSpec(shape, lambda r, s: (0,) * len(shape))


def grouped_product(scalars, pieces, block, n_fold, groups, *, bounds, irreps, halves, window, me):
    n_rows, depth = pieces[0].shape
    width = block.shape[2]
    n_i = groups // halves
    share = (n_i * n_rows // n_fold, halves * width)
    shape = (n_fold, share[0] + 8, share[1])
    return pl.pallas_call(
        functools.partial(
            grouped_kernel, bounds=bounds, irreps=irreps, halves=halves, window=window, me=me
        ),
        out_shape=jax.ShapeDtypeStruct(shape, jnp.int16),
        grid_spec=pltpu.PrefetchScalarGridSpec(
            num_scalar_prefetch=1,
            grid=(irreps,),
            in_specs=[pl.BlockSpec(memory_space=pl.ANY)] * len(pieces)
            + [pl.BlockSpec((1, depth, width), lambda r, s: (r, 0, 0))],
            out_specs=whole(shape),
            scratch_shapes=[
                pltpu.VMEM((groups, n_rows, depth), BF16),
                pltpu.VMEM((groups * window, depth), BF16),
                pltpu.VMEM((groups, n_rows, width), F32),
                pltpu.VMEM(share, F32),
                pltpu.SemaphoreType.DMA((len(pieces),)),
            ],
        ),
        compiler_params=pltpu.CompilerParams(vmem_limit_bytes=48 * 2**20),
        cost_estimate=pl.CostEstimate(
            flops=2 * irreps * groups * window * depth * width, bytes_accessed=13 * 2**20, transcendentals=0
        ),
    )(scalars, *pieces, block)


def body(amplitudes, cycle_block, occ_sizes, vir_sizes, window_i, window_occ):
    irreps = occ_sizes.shape[0]
    n_fold, n_pair = lax.axis_size("fold"), lax.axis_size("pair")
    fold, pair = lax.axis_index("fold"), lax.axis_index("pair")
    c_local, occ_total, j_local, vir_total = cycle_block.shape
    n_i, k_local, a_local, _ = amplitudes.shape
    vmax, omax = vir_total // 4, occ_total // 4
    halves = n_pair // n_i
    a_part = a_local // halves

    labels, places, all_starts = irrep_labels(jnp.stack([occ_sizes, vir_sizes]), vir_total)
    occ, vir, vir_place = labels[0, :occ_total], labels[1], places[1]
    occ_starts, starts = all_starts[0], all_starts[1]
    to_place = one_hot_rows(vir_place, vmax)
    kappas = omax + 2 - omax % 2
    k_from = jnp.minimum(occ_starts[:irreps] // 2 * 2, occ_total - kappas)
    own_from = jnp.where(occ[:, None] == jnp.arange(irreps)[None, :], k_from[None, :], 0)
    kappa = jnp.arange(occ_total, dtype=jnp.int32) - jnp.sum(own_from, axis=1)
    to_kappa = one_hot_rows(kappa, kappas)
    own_vir = lax.dynamic_slice_in_dim(vir, fold * c_local, c_local)
    k_own = lax.dynamic_slice_in_dim(occ, pair * k_local, k_local)
    i_labels = label_lookup(window_i, occ, occ_total)
    j_labels = label_lookup(lax.dynamic_slice_in_dim(window_occ, pair * j_local, j_local), occ, occ_total)

    narrow = narrow_c(
        jnp.concatenate([i_labels, k_own]), amplitudes, own_vir[:, None], vir[None, :], to_place, halves
    )
    narrow = lax.all_to_all(narrow, "pair", split_axis=0, concat_axis=0, tiled=True)
    cycle = cycle_block.transpose(2, 1, 0, 3).reshape(j_local, occ_total // 2, 2 * c_local, vir_total)
    narrow, cycle = lax.optimization_barrier((narrow, cycle))

    i_mine = lax.dynamic_index_in_dim(i_labels, pair // halves, keepdims=False)
    a_mine = lax.dynamic_slice_in_dim(vir, fold * a_local + (pair % halves) * a_part, a_part)
    x = (i_mine ^ occ[:, None] ^ a_mine[None, :]).reshape(n_pair, k_local * a_part, 1)
    a_rows = -(-a_part // 8) * 8
    room = -(-k_local * a_part // 16) * 16
    row = jnp.arange(kappas * a_rows, dtype=jnp.int32)[:, None]
    k_kappa = jnp.repeat(kappa, a_part).reshape(n_pair, -1)
    k_kappa = jnp.pad(k_kappa, ((0, 0), (0, room - k_kappa.shape[1])), constant_values=-1).reshape(1, -1)
    column = jnp.arange(n_pair * room, dtype=jnp.int32)[None, :] % room % a_part
    to_row = ((row // a_rows == k_kappa) & (row % a_rows == column)).astype(BF16)
    short = narrow_k(narrow, to_place, x, vir[None, :], to_row, n_fold, a_part, c_local)
    short = lax.all_to_all(short, "fold", split_axis=0, concat_axis=0, tiled=True)

    code = (vir * vmax + vir_place)[None, :, None]
    spots = jnp.arange(irreps * vmax, dtype=jnp.int32).reshape(irreps, 1, vmax)
    picks = (code == spots).astype(BF16)
    short, picks = lax.optimization_barrier((short, picks))
    inside = starts % a_local
    bounds = [starts // a_local * a_part + jnp.clip(inside - h * a_part, 0, a_part) for h in range(halves)]
    scalars = jnp.concatenate([i_labels, k_from // 2, j_labels] + bounds + [own_vir, pair[None]]).astype(jnp.int32)
    low = n_i + irreps + j_local
    me = low + halves * (irreps + 1) + c_local
    c_label = jnp.broadcast_to(jnp.tile(own_vir.astype(F32), 2)[:, None], (2 * c_local, vir_total)).astype(BF16)
    blocks = class_blocks(
        scalars, cycle, c_label, picks, n_i=n_i, irreps=irreps, owns=low + halves * (irreps + 1), k_pairs=kappas // 2
    )
    short = short.reshape(n_fold * a_part, kappas * c_local)
    lhs, blocks = gather_pieces(short, blocks, n_pair)

    most = min(vmax, -(-vmax // a_local) * a_part)
    window = min(-(-(most + 15) // 16) * 16, n_fold * a_part)
    coded = grouped_product(
        scalars, lhs, blocks, n_fold, n_pair, bounds=low, irreps=irreps, halves=halves, window=window, me=me
    )
    coded = lax.all_to_all(coded, "fold", split_axis=0, concat_axis=0, tiled=True).astype(F32)
    shares = coded[:, :-8] * (jnp.exp2(coded[:, -8:-7] * 0.25) / TOP)
    total = jnp.sum(shares, axis=0).astype(BF16).reshape(n_i, a_part, halves, j_local, vmax)
    total = total.transpose(0, 2, 1, 3, 4).reshape(n_i, a_local, j_local, vmax)
    spread_b = pick(total, "iajt,tb->iajb", to_place)
    x = i_labels[:, None, None] ^ own_vir[None, :, None] ^ j_labels[None, None, :]
    return jnp.where(x[..., None] == vir, spread_b, jnp.zeros_like(spread_b))


def solution(mesh):
    placed = (P(None, "pair", "fold", None), P("fold", None, "pair", None), P(), P(), P(), P())
    return jax.shard_map(
        body, mesh=mesh, in_specs=placed, out_specs=P(None, "fold", "pair", None), check_vma=False
    )
```
